128 devices in a mesh: seq: 32 (over y, x, core), exp: 4 (over z).
Axes of the slice: x: 4, y: 4, z: 4, core: 2. Of those that a mesh axis runs over, the one named last changes fastest.
Arguments:
- inner: bfloat16 [4096, 8192], P('seq', 'exp'), may hold values from -3 to 3
- gate_in: bfloat16 [4096, 8192], P('seq', 'exp'), may hold values from -3 to 3
- w_low: bfloat16 [8192, 512], P('exp'), may hold values from -0.0625 to 0.0625
- w_state: bfloat16 [8192, 32], P('exp'), may hold values from -0.0078125 to 0.0078125
- w_dt: bfloat16 [512, 8192], P(None, 'exp'), may hold values from -0.25 to 0.25
- dt_bias: float32 [8192], P('exp'), may hold values from -2 to 1
- decay_rate: float32 [8192, 16], P('exp'), may hold values from 5e-06 to 0.08
- skip_gain: float32 [8192], P('exp'), may hold values from 0.1 to 1.9
- w_router: bfloat16 [8192, 16], P('exp'), may hold values from -0.125 to 0.125
- expert_ids: int32 [4096, 2], P('seq'), may hold values from 0 to 15, all different within a row; in each aligned block of 128 rows (0 to 127, 128 to 255, ...) at most 24 rows name the same one
- w_gate: bfloat16 [4, 8192, 12288], P('exp', None, 'seq'), may hold values from -0.0625 to 0.0625
- w_up: bfloat16 [4, 8192, 12288], P('exp', None, 'seq'), may hold values from -0.0625 to 0.0625
- w_down: bfloat16 [4, 12288, 8192], P('exp', 'seq'), may hold values from -0.0546875 to 0.0546875
Outputs:
- layer_out: float32 [4096, 8192], P('seq', 'exp')
The draws below stay inside these ranges and needn't reach their ends.
Inputs may be any that keep to these rules, and one draw needn't show every extreme that they name: `expert_ids`: each row names two different experts; among the 128 rows of one shard no expert is named more than 24 times.
All inputs are finite; a program needn't handle non-finite values.
Results may differ from the reference program's by a relative error of at most 0.022.
Values may be sent and summed in bfloat16 or wider, within the bound.
A program may use at most 192 MiB of HBM per device.

```python
import math
import jax
import jax.numpy as jnp
import numpy as np
from jax import lax

DI = 8192
FFW = 12288
R = 512
N = 16
NE = 16
TS = 128
E_WIN = 4
CAP = 24
TOKENS = 4096
N_SEQ = 32


def block_levels(stream_key, shape, pieces, low, largest):
    gain = 1.0
    for position, parts in pieces:
        heights = jax.random.uniform(jax.random.fold_in(jax.random.fold_in(stream_key, 6), position), (parts,), jnp.float32, low / len(pieces), largest / len(pieces))
        gain = gain * jnp.repeat(jnp.exp(heights), shape[position] // parts).reshape((-1,) + (1,) * (len(shape) - 1 - position))
    return gain


def routed_block(rng, own, number, rows, amount, top, most, lean):
    sequence = jax.random.permutation(rng, amount)
    crowded, ordinary = portions_of(amount, rows * top, most, lean, True), portions_of(amount, rows * top, most, lean, False)
    places = jnp.arange(amount)

    def named(lengths, rotation):
        used = int((lengths > 0).sum())
        fixed = max(1, used // 4)
        passed = fixed + (places - fixed + rotation * (used - fixed)) % max(1, amount - fixed)
        return jnp.zeros((amount,), jnp.int32).at[sequence[jnp.where(places < fixed, places, passed)]].set(jnp.asarray(lengths, jnp.int32))

    lengths = jnp.where(number % 4 == 0, named(crowded, number // 4), named(ordinary, number - number // 4 - 1))
    mixed = jax.random.permutation(jax.random.fold_in(own, 3), amount)
    giver, receiver = mixed[0:amount // 2 * 2:2], mixed[1:amount // 2 * 2:2]
    margin = jnp.minimum(lengths[giver] - 1, most - lengths[receiver]) // 2
    margin = jnp.where((giver == sequence[0]) | (receiver == sequence[0]) | (lengths[receiver] == 0), 0, jnp.maximum(margin, 0))
    passed = jax.random.randint(jax.random.fold_in(own, 4), (amount // 2,), 0, 1 << 20) % (margin + 1)
    lengths = lengths.at[giver].add(-passed).at[receiver].add(passed)
    members = jnp.searchsorted(jnp.cumsum(lengths), jnp.arange(rows * top), side="right").astype(jnp.int32)
    listing = members.reshape(top, rows).T
    listing = listing[jax.random.permutation(jax.random.fold_in(own, 1), rows)]
    rotation = jax.random.randint(jax.random.fold_in(own, 2), (rows, 1), 0, top)
    return jnp.take_along_axis(listing, (jnp.arange(top)[None, :] + rotation) % top, axis=1)


def portions_of(amount, total, bound, skew, full):
    loads = [(1 << 20) // math.isqrt(standing ** skew) + 1 for standing in range(1, amount + 1)]
    largest = bound if full else min(bound, max(-(-total // amount), total * loads[0] // sum(loads)))
    least = 1 if total - largest >= amount - 1 else 0
    holding, rest = [largest] + [least] * (amount - 1), total - largest - least * (amount - 1)
    while rest > 0:
        free = [i for i in range(1, amount) if holding[i] < largest] or [i for i in range(1, amount) if holding[i] < bound]
        whole, left = sum([loads[i] for i in free]), rest
        for i in free:
            extra = min(bound - holding[i], max(1, left * loads[i] // whole), rest)
            holding[i] = holding[i] + extra
            rest = rest - extra
    return np.array(holding)


def noise(stream_key, extent, spread, most, cuts=(), kind=jnp.bfloat16):
    array = jax.random.normal(stream_key, extent, jnp.float32) * spread
    if len(cuts) > 0:
        array = block_levels(stream_key, extent, cuts, -0.22, 0.18) * array
    return jnp.clip(array, min=-most, max=most).astype(kind)


def setup_inputs(seed: int = 0) -> dict:
    seeds = jax.random.split(jax.random.key(seed), 14)
    inner = noise(seeds[0], (TOKENS, DI), 1.0, 3.0, ((0, 32), (1, 4)))
    gate_in = noise(seeds[1], (TOKENS, DI), 1.0, 3.0, ((0, 32), (1, 4)))
    w_low = noise(seeds[2], (DI, R), DI ** -0.5, 0.0625, ((0, 4),))
    w_state = noise(seeds[3], (DI, 2 * N), (DI * 64) ** -0.5, 0.0078125, ((0, 4),))
    w_dt = noise(seeds[4], (R, DI), R ** -0.5, 0.25, ((1, 4),))
    dt_bias = jnp.clip(-2.0 + 3.0 * jax.random.uniform(seeds[5], (DI,), jnp.float32) ** block_levels(seeds[5], (DI,), ((0, 4),), -0.2, 0.2), -2.0, 1.0)
    decay_rate = jnp.clip(jnp.exp(math.log(0.08) - 9.680344 * jax.random.uniform(seeds[6], (DI, N), jnp.float32) ** block_levels(seeds[6], (DI, N), ((0, 4),), -0.2, 0.2)), 4.999999873689376e-06, 0.08)
    skip_gain = jnp.clip(1.0 + 0.18 * jax.random.normal(seeds[7], (DI,), jnp.float32), 0.1, 1.9)
    w_router = noise(seeds[8], (DI, NE), (DI // 4) ** -0.5, 0.125, ((0, 4),))
    expert_ids_keys = jax.random.split(jax.random.fold_in(seeds[9], 1), TOKENS // TS)
    expert_ids_turns = jax.random.permutation(jax.random.fold_in(seeds[9], 3), TOKENS // TS)
    expert_ids = jax.vmap(lambda own, number: routed_block(jax.random.fold_in(seeds[9], 2), own, number, TS, NE, 2, CAP, 2))(expert_ids_keys, expert_ids_turns).reshape((TOKENS, 2))
    w_gate = noise(seeds[10], (E_WIN, DI, FFW), DI ** -0.5, 0.0625, ((0, 4), (2, 32)))
    w_up = noise(seeds[11], (E_WIN, DI, FFW), DI ** -0.5, 0.0625, ((0, 4), (2, 32)))
    w_down = noise(seeds[12], (E_WIN, FFW, DI), FFW ** -0.5, 0.0546875, ((0, 4), (1, 32)))
    return dict(inner=inner, gate_in=gate_in, w_low=w_low, w_state=w_state, w_dt=w_dt, dt_bias=dt_bias, decay_rate=decay_rate, skip_gain=skip_gain, w_router=w_router, expert_ids=expert_ids, w_gate=w_gate, w_up=w_up, w_down=w_down)


def reference(inner, gate_in, w_low, w_state, w_dt, dt_bias, decay_rate, skip_gain, w_router, expert_ids, w_gate, w_up, w_down):
    low = jnp.dot(inner, w_low, preferred_element_type=jnp.float32)
    state_maps = jnp.dot(inner, w_state, preferred_element_type=jnp.float32)
    input_map = state_maps[:, :N]
    output_map = state_maps[:, N:]
    step_size = jax.nn.softplus(jnp.dot(low.astype(jnp.bfloat16), w_dt, preferred_element_type=jnp.float32) + dt_bias)
    signal = inner.astype(jnp.float32)

    def advance(carried, inputs):
        delta_row, value_row, input_row, output_row = inputs
        carried = jnp.exp(-delta_row[:, None] * decay_rate) * carried + (delta_row * value_row)[:, None] * input_row[None, :]
        return carried, jnp.sum(carried * output_row[None, :], axis=1)

    _, scanned = lax.scan(advance, jnp.zeros((DI, N), jnp.float32), (step_size, signal, input_map, output_map))
    mixer_out = ((scanned + skip_gain * signal) * jax.nn.silu(gate_in.astype(jnp.float32))).astype(jnp.bfloat16)

    logits = jnp.dot(mixer_out, w_router, preferred_element_type=jnp.float32)
    chosen = jnp.take_along_axis(logits, expert_ids, axis=1)
    shares = 1.0 / (1.0 + jnp.exp(chosen[:, ::-1] - chosen))

    window = jnp.arange(E_WIN, dtype=jnp.int32)
    hit_table = (expert_ids[:, :, None] == window[None, None, :]).astype(jnp.int32)
    load_count = jnp.sum(hit_table, axis=1).reshape(N_SEQ, TS, E_WIN)
    earlier = (jnp.cumsum(load_count, axis=1) - load_count).reshape(TOKENS, E_WIN)
    slot_index = jnp.sum(hit_table * earlier[:, None, :], axis=2)
    inside = expert_ids < E_WIN
    shard_of = jnp.arange(TOKENS, dtype=jnp.int32) // TS
    spot = shard_of[:, None] * CAP + slot_index
    target = jnp.where(inside, expert_ids, E_WIN)
    rows = jnp.zeros((E_WIN, N_SEQ * CAP, DI), jnp.bfloat16).at[target, spot].set(
        jnp.broadcast_to(mixer_out[:, None, :], (TOKENS, 2, DI)), mode="drop")

    def expert(packed):
        block_rows, gate_matrix, up_matrix, down_matrix = packed
        hidden = (jax.nn.silu(jnp.dot(block_rows, gate_matrix, preferred_element_type=jnp.float32))
                  * jnp.dot(block_rows, up_matrix, preferred_element_type=jnp.float32)).astype(jnp.bfloat16)
        hidden_blocks = hidden.reshape(N_SEQ * CAP, N_SEQ, FFW // N_SEQ).transpose(1, 0, 2)
        down_blocks = down_matrix.reshape(N_SEQ, FFW // N_SEQ, DI)

        def accumulate(running, blocks):
            partial_value = lax.optimization_barrier(jnp.dot(blocks[0], blocks[1], preferred_element_type=jnp.float32).astype(jnp.bfloat16))
            return running + partial_value.astype(jnp.float32), None

        running, _ = lax.scan(accumulate, jnp.zeros((N_SEQ * CAP, DI), jnp.float32), (hidden_blocks, down_blocks))
        return running.astype(jnp.bfloat16)

    expert_out = lax.map(expert, (rows, w_gate, w_up, w_down))
    gathered = expert_out[jnp.minimum(expert_ids, E_WIN - 1), spot]
    contrib = jnp.where(inside[:, :, None], shares[:, :, None] * gathered.astype(jnp.float32), 0.0)
    return mixer_out.astype(jnp.float32) + jnp.sum(contrib, axis=1)
```

```python
import functools

import jax
import jax.numpy as jnp
from jax import lax
from jax.experimental import pallas as pl
from jax.experimental.pallas import tpu as pltpu
from jax.sharding import PartitionSpec as P

N = 16
NE = 16
CAP = 24
LANES = 128
LOG2E = 1.4426950408889634
VMEM_LIMIT = 60 * 1024 * 1024


def softplus(v):
    return jnp.maximum(v, 0.0) + jnp.log1p(jnp.exp(-jnp.abs(v)))


def spread(ref, cols):
    tokens = cols.shape[0]
    for n in range(N):
        ref[pl.ds(n, tokens, stride=N), :] = jnp.broadcast_to(
            cols[:, n : n + 1], (tokens, LANES)
        )


def first_pass_kernel(low_ref, wdt_ref, bias_ref, inner_ref, rate_ref, bmap_ref,
                      dt_ref, u_ref, tiles_ref, b_s):
    tokens, channels = inner_ref.shape
    tiles = channels // LANES
    low = low_ref[...]
    for j in range(channels // 256):
        cols = pl.ds(j * 256, 256)
        dt = softplus(
            jnp.dot(low, wdt_ref[:, cols], preferred_element_type=jnp.float32)
            + bias_ref[:, cols]
        )
        u = dt * inner_ref[:, cols].astype(jnp.float32)
        for k in range(2):
            part = slice(k * LANES, (k + 1) * LANES)
            dt_ref[pl.ds(2 * j + k, tokens, stride=tiles), :] = dt[:, part]
            u_ref[pl.ds(2 * j + k, tokens, stride=tiles), :] = u[:, part]
    spread(b_s, bmap_ref[...])
    for half in range(2):
        rate = [rate_ref[n, half * 8 : half * 8 + 8, :] for n in range(N)]

        def step(t, carry):
            total, h = carry
            at = pl.multiple_of(t * tiles + half * 8, 8)
            dt = dt_ref[pl.ds(at, 8), :]
            u = u_ref[pl.ds(at, 8), :]
            new = []
            for n in range(N):
                b = b_s[pl.ds(t * N + n, 1), :]
                new.append(jnp.exp2(dt * rate[n]) * h[n] + u * b)
            return total + dt, tuple(new)

        zero = jnp.zeros((8, LANES), jnp.float32)
        total, h = lax.fori_loop(0, tokens, step, (zero, (zero,) * N), unroll=4)
        for n in range(N):
            tiles_ref[2 * n + half, 0] = jnp.exp2(total * rate[n])
            tiles_ref[2 * n + half, 1] = h[n]


def second_pass_kernel(dt_ref, u_ref, rate_ref, bmap_ref, cmap_ref, h0_ref, inner_ref, gate_ref,
                       skip_ref, wr_ref, mixer_ref, logits_ref, b_s, c_s, y_s):
    tokens, channels = inner_ref.shape
    tiles = channels // LANES
    spread(b_s, bmap_ref[...])
    spread(c_s, cmap_ref[...])
    for half in range(2):
        rate = [rate_ref[n, half * 8 : half * 8 + 8, :] for n in range(N)]

        def step(t, h):
            at = pl.multiple_of(t * tiles + half * 8, 8)
            dt = dt_ref[pl.ds(at, 8), :]
            u = u_ref[pl.ds(at, 8), :]
            new = []
            y = None
            for n in range(N):
                b = b_s[pl.ds(t * N + n, 1), :]
                c = c_s[pl.ds(t * N + n, 1), :]
                new.append(jnp.exp2(dt * rate[n]) * h[n] + u * b)
                y = new[n] * c if y is None else y + new[n] * c
            y_s[pl.ds(at, 8), :] = y
            return tuple(new)

        lax.fori_loop(0, tokens, step, tuple(h0_ref[2 * n + half] for n in range(N)), unroll=4)
    for j in range(tiles):
        cols = pl.ds(j * LANES, LANES)
        y = y_s[pl.ds(j, tokens, stride=tiles), :]
        gate = gate_ref[:, cols].astype(jnp.float32)
        value = (y + skip_ref[:, cols] * inner_ref[:, cols].astype(jnp.float32)) * (
            gate / (1.0 + jnp.exp(-gate))
        )
        mixer_ref[:, cols] = value.astype(jnp.bfloat16)
    logits_ref[...] = jnp.dot(mixer_ref[...], wr_ref[...], preferred_element_type=jnp.float32)


def mixer(rank_sum, state_sum, inner, gate_in, w_dt, dt_bias, decay_rate, skip_gain, w_router):
    tokens, channels = inner.shape
    tiles = channels // LANES
    count, mine = lax.axis_size("seq"), lax.axis_index("seq")
    f32 = jnp.float32
    rate = (decay_rate * -LOG2E).T.reshape(N, tiles, LANES)
    bmap, cmap = state_sum[:, :N], state_sum[:, N:]
    rows = jax.ShapeDtypeStruct((tokens * tiles, LANES), f32)
    params = pltpu.CompilerParams(vmem_limit_bytes=VMEM_LIMIT)
    dt, u, ends = pl.pallas_call(
        first_pass_kernel,
        out_shape=(rows, rows, jax.ShapeDtypeStruct((2 * N, 2, 8, LANES), f32)),
        scratch_shapes=[pltpu.VMEM((tokens * N, LANES), f32)],
        compiler_params=params,
    )(rank_sum.astype(jnp.bfloat16), w_dt, dt_bias[None], inner, rate, bmap)
    heard = lax.all_to_all(ends, "seq", split_axis=0, concat_axis=0, tiled=True)
    carry = jnp.zeros((8, LANES), f32)
    carries = []
    for s in range(count):
        carries.append(carry)
        carry = heard[s, 0] * carry + heard[s, 1]
    h0 = lax.all_to_all(jnp.stack(carries), "seq", split_axis=0, concat_axis=0, tiled=True)
    return pl.pallas_call(
        second_pass_kernel,
        out_shape=(
            jax.ShapeDtypeStruct((tokens, channels), jnp.bfloat16),
            jax.ShapeDtypeStruct((tokens, NE), f32),
        ),
        scratch_shapes=[pltpu.VMEM((tokens * N, LANES), f32)] * 2
        + [pltpu.VMEM((tokens * tiles, LANES), f32)],
        compiler_params=params,
    )(dt, u, rate, bmap, cmap, h0, inner, gate_in, skip_gain[None], w_router)


def on_device(
    inner,
    gate_in,
    w_low,
    w_state,
    w_dt,
    dt_bias,
    decay_rate,
    skip_gain,
    w_router,
    expert_ids,
    w_gate,
    w_up,
    w_down,
):
    tokens, channels = inner.shape
    experts = lax.axis_size("exp")
    rank_part = jnp.dot(inner, w_low, preferred_element_type=jnp.float32)
    state_part = jnp.dot(inner, w_state, preferred_element_type=jnp.float32)
    rank_sum, state_sum = lax.psum((rank_part, state_part), "exp")
    mixer_out, logits_part = mixer(
        rank_sum, state_sum, inner, gate_in, w_dt, dt_bias, decay_rate, skip_gain, w_router
    )
    logits = lax.psum(logits_part, "exp")
    catalog = jnp.arange(NE, dtype=jnp.int32)
    chosen = jnp.sum(
        jnp.where(expert_ids[:, :, None] == catalog[None, None, :], logits[:, None, :], 0.0), axis=2
    )
    shares = 1.0 / (1.0 + jnp.exp(chosen[:, ::-1] - chosen))
    window = jnp.arange(experts, dtype=jnp.int32)
    hit_table = (expert_ids[:, :, None] == window[None, None, :]).astype(jnp.int32)
    load_count = jnp.sum(hit_table, axis=1)
    earlier = jnp.cumsum(load_count, axis=0) - load_count
    slot_index = jnp.sum(hit_table * earlier[:, None, :], axis=2)
    matches = (slot_index[:, :, None] == jnp.arange(CAP, dtype=jnp.int32)[None, None, :]).astype(
        jnp.float32
    )
    picked = hit_table.astype(jnp.float32)
    selector = jnp.einsum("tke,tkc->ect", picked, matches).astype(jnp.bfloat16)
    outgoing = jnp.einsum(
        "ect,td->ecd", selector, mixer_out, preferred_element_type=jnp.float32
    ).astype(jnp.bfloat16)
    arrived = lax.all_to_all(outgoing, "exp", split_axis=0, concat_axis=2, tiled=True)[0]
    gate_weights = w_gate[0]
    up_weights = w_up[0]
    down_weights = w_down[0]
    row_piece = lax.all_gather(arrived, "seq", axis=0, tiled=True)
    hidden = (
        jax.nn.silu(jnp.dot(row_piece, gate_weights, preferred_element_type=jnp.float32))
        * jnp.dot(row_piece, up_weights, preferred_element_type=jnp.float32)
    ).astype(jnp.bfloat16)
    summed = lax.psum_scatter(
        lax.optimization_barrier(
            jnp.dot(hidden, down_weights, preferred_element_type=jnp.float32).astype(jnp.bfloat16)
        )
        .astype(jnp.float32)
        .astype(jnp.bfloat16),
        "seq",
        scatter_dimension=0,
        tiled=True,
    )
    returned = lax.all_to_all(summed[None], "exp", split_axis=2, concat_axis=0, tiled=True)
    weighting = jnp.einsum(
        "tk,tke,tkc->tec", shares, picked, matches, precision=lax.Precision.HIGHEST
    )
    combined = jnp.dot(
        weighting.reshape(tokens, experts * CAP),
        returned.reshape(experts * CAP, channels).astype(jnp.float32),
        precision=lax.Precision.HIGHEST,
    )
    return mixer_out.astype(jnp.float32) + combined


def solution(mesh):
    in_specs = (
        P("seq", "exp"),
        P("seq", "exp"),
        P("exp", None),
        P("exp", None),
        P(None, "exp"),
        P("exp"),
        P("exp", None),
        P("exp"),
        P("exp", None),
        P("seq", None),
        P("exp", None, "seq"),
        P("exp", None, "seq"),
        P("exp", "seq", None),
    )
    out_specs = P("seq", "exp")
    return jax.shard_map(
        on_device, mesh=mesh, in_specs=in_specs, out_specs=out_specs, check_vma=False
    )
```

```python
import functools

import jax
import jax.numpy as jnp
from jax import lax
from jax.experimental import pallas as pl
from jax.experimental.pallas import tpu as pltpu
from jax.sharding import PartitionSpec as P

N = 16
NE = 16
CAP = 24
LANES = 128
LOG2E = 1.4426950408889634
VMEM_LIMIT = 60 * 1024 * 1024


def softplus(v):
    return jnp.maximum(v, 0.0) + jnp.log1p(jnp.exp(-jnp.abs(v)))


def spread(ref, cols):
    tokens = cols.shape[0]
    for n in range(N):
        ref[pl.ds(n, tokens, stride=N), :] = jnp.broadcast_to(
            cols[:, n : n + 1], (tokens, LANES)
        )


def first_pass_kernel(low_ref, wdt_ref, bias_ref, inner_ref, rate_ref, bmap_ref,
                      dt_ref, u_ref, tiles_ref, b_s):
    tokens, channels = inner_ref.shape
    tiles = channels // LANES
    low = low_ref[...]
    for j in range(channels // 256):
        cols = pl.ds(j * 256, 256)
        dt = softplus(
            jnp.dot(low, wdt_ref[:, cols], preferred_element_type=jnp.float32)
            + bias_ref[:, cols]
        )
        u = dt * inner_ref[:, cols].astype(jnp.float32)
        for k in range(2):
            part = slice(k * LANES, (k + 1) * LANES)
            dt_ref[pl.ds(2 * j + k, tokens, stride=tiles), :] = dt[:, part]
            u_ref[pl.ds(2 * j + k, tokens, stride=tiles), :] = u[:, part]
    spread(b_s, bmap_ref[...])
    for half in range(2):
        rate = [rate_ref[n, half * 8 : half * 8 + 8, :] for n in range(N)]

        def step(t, carry):
            total, h = carry
            at = pl.multiple_of(t * tiles + half * 8, 8)
            dt = dt_ref[pl.ds(at, 8), :]
            u = u_ref[pl.ds(at, 8), :]
            new = []
            for n in range(N):
                b = b_s[pl.ds(t * N + n, 1), :]
                new.append(jnp.exp2(dt * rate[n]) * h[n] + u * b)
            return total + dt, tuple(new)

        zero = jnp.zeros((8, LANES), jnp.float32)
        total, h = lax.fori_loop(0, tokens, step, (zero, (zero,) * N), unroll=4)
        for n in range(N):
            tiles_ref[2 * n + half, 0] = jnp.exp2(total * rate[n])
            tiles_ref[2 * n + half, 1] = h[n]


def second_pass_kernel(dt_ref, u_ref, rate_ref, bmap_ref, cmap_ref, h0_ref, inner_ref, gate_ref,
                       skip_ref, wr_ref, mixer_ref, logits_ref, b_s, c_s, y_s):
    tokens, channels = inner_ref.shape
    tiles = channels // LANES
    spread(b_s, bmap_ref[...])
    spread(c_s, cmap_ref[...])
    for half in range(2):
        rate = [rate_ref[n, half * 8 : half * 8 + 8, :] for n in range(N)]

        def step(t, h):
            at = pl.multiple_of(t * tiles + half * 8, 8)
            dt = dt_ref[pl.ds(at, 8), :]
            u = u_ref[pl.ds(at, 8), :]
            new = []
            y = None
            for n in range(N):
                b = b_s[pl.ds(t * N + n, 1), :]
                c = c_s[pl.ds(t * N + n, 1), :]
                new.append(jnp.exp2(dt * rate[n]) * h[n] + u * b)
                y = new[n] * c if y is None else y + new[n] * c
            y_s[pl.ds(at, 8), :] = y
            return tuple(new)

        lax.fori_loop(0, tokens, step, tuple(h0_ref[2 * n + half] for n in range(N)), unroll=4)
    for j in range(tiles):
        cols = pl.ds(j * LANES, LANES)
        y = y_s[pl.ds(j, tokens, stride=tiles), :]
        gate = gate_ref[:, cols].astype(jnp.float32)
        value = (y + skip_ref[:, cols] * inner_ref[:, cols].astype(jnp.float32)) * (
            gate / (1.0 + jnp.exp(-gate))
        )
        mixer_ref[:, cols] = value.astype(jnp.bfloat16)
    logits_ref[...] = jnp.dot(mixer_ref[...], wr_ref[...], preferred_element_type=jnp.float32)


def mixer(rank_sum, state_sum, inner, gate_in, w_dt, dt_bias, decay_rate, skip_gain, w_router):
    tokens, channels = inner.shape
    tiles = channels // LANES
    count, mine = lax.axis_size("seq"), lax.axis_index("seq")
    f32 = jnp.float32
    rate = (decay_rate * -LOG2E).T.reshape(N, tiles, LANES)
    bmap, cmap = state_sum[:, :N], state_sum[:, N:]
    rows = jax.ShapeDtypeStruct((tokens * tiles, LANES), f32)
    params = pltpu.CompilerParams(vmem_limit_bytes=VMEM_LIMIT)
    dt, u, ends = pl.pallas_call(
        first_pass_kernel,
        out_shape=(rows, rows, jax.ShapeDtypeStruct((2 * N, 2, 8, LANES), f32)),
        scratch_shapes=[pltpu.VMEM((tokens * N, LANES), f32)],
        compiler_params=params,
    )(rank_sum.astype(jnp.bfloat16), w_dt, dt_bias[None], inner, rate, bmap)
    heard = lax.all_to_all(ends, "seq", split_axis=0, concat_axis=0, tiled=True)
    carry = jnp.zeros((8, LANES), f32)
    carries = []
    for s in range(count):
        carries.append(carry)
        carry = heard[s, 0] * carry + heard[s, 1]
    h0 = lax.all_to_all(jnp.stack(carries), "seq", split_axis=0, concat_axis=0, tiled=True)
    return pl.pallas_call(
        second_pass_kernel,
        out_shape=(
            jax.ShapeDtypeStruct((tokens, channels), jnp.bfloat16),
            jax.ShapeDtypeStruct((tokens, NE), f32),
        ),
        scratch_shapes=[pltpu.VMEM((tokens * N, LANES), f32)] * 2
        + [pltpu.VMEM((tokens * tiles, LANES), f32)],
        compiler_params=params,
    )(dt, u, rate, bmap, cmap, h0, inner, gate_in, skip_gain[None], w_router)


ROWS = 2 * CAP
WIDE = 1024
SIDE = 4


def expert_kernel(rows_ref, gate_ref, up_ref, down_ref, out_ref,
                  x, w_in, w_out, acc, hid, first, q, r1, r2, done,
                  w_sem, first_sem, ag_send, ag_recv, core_send, core_recv,
                  q_send, q_recv, r1_send, r1_recv, r2_send, r2_recv, done_sem):
    seq = lax.axis_index("seq")
    c = seq % 2
    chip = seq // 2
    f = w_out.shape[1]
    f32 = jnp.float32
    p1 = (1 - c) * (chip % SIDE) + c * (chip // SIDE)
    p2 = (1 - c) * (chip // SIDE) + c * (chip % SIDE)
    me = p2 * SIDE + p1

    def at(i1, i2, core=None):
        where = (1 - c) * (i2 * SIDE + i1) + c * (i1 * SIDE + i2)
        return {"seq": where * 2 + (c if core is None else core)}

    sibling = at(p1, p2, 1 - c)
    right1, left1 = at((p1 + 1) % SIDE, p2), at((p1 + 3) % SIDE, p2)
    right2, left2 = at(p1, (p2 + 1) % SIDE), at(p1, (p2 + 3) % SIDE)

    def remote(src, dst, send, recv, device):
        return pltpu.make_async_remote_copy(
            src_ref=src, dst_ref=dst, send_sem=send, recv_sem=recv,
            device_id=device, device_id_type=pl.DeviceIdType.MESH)

    def weights_in(o, n):
        return pltpu.make_async_copy(
            (gate_ref, up_ref)[n].at[0, pl.ds(o * WIDE, WIDE), :], w_in.at[o, :, pl.ds(n * f, f)], w_sem.at[n, o])

    def weights_out(o):
        return pltpu.make_async_copy(down_ref.at[0, :, pl.ds(o * WIDE, WIDE)], w_out.at[o], w_sem.at[2, o])

    for o in range(8):
        for n in range(2):
            weights_in((4 * c + o) % 8, n).start()
    for o in range(8):
        weights_out(o).start()

    barrier = pltpu.get_barrier_semaphore()
    for peer in (sibling, right1, left1, right2, left2):
        pl.semaphore_signal(barrier, inc=1, device_id=peer, device_id_type=pl.DeviceIdType.MESH)
    pl.semaphore_wait(barrier, 5)

    swap = remote(rows_ref.at[pl.ds(4 * (1 - c), 4)], first, first_sem.at[0], first_sem.at[1], sibling)
    swap.start()
    swap.wait()
    for k in range(4):
        x[c, me, k] = rows_ref[4 * c + k] + first[k]

    sent = []

    def spot(d1, d2):
        return ((p2 + 4 - d2) % SIDE) * SIDE + (p1 + 4 - d1) % SIDE

    def whole(d1, d2, n1, n2, device, slot):
        i = spot(d1, d2)
        copy = remote(x.at[c, i], x.at[c, i], ag_send.at[slot], ag_recv.at[n2 * 4 + n1, 0], device)
        copy.start()
        sent.append((ag_send, slot, 4))

    def pair(d1, d2, n1, n2, device, slot, k):
        i = spot(d1, d2)
        part = x.at[c, i, pl.ds(2 * k, 2)]
        copy = remote(part, part, ag_send.at[slot], ag_recv.at[n2 * 4 + n1, k], device)
        copy.start()
        sent.append((ag_send, slot, 2))

    def arrive(d1, d2):
        i = spot(d1, d2)
        if d2 == 2 or (d2 == 0 and d1 == 2):
            for k in range(2):
                part = x.at[c, i, pl.ds(2 * k, 2)]
                remote(part, part, ag_send.at[0], ag_recv.at[d2 * 4 + d1, k], sibling).wait_recv()
        else:
            remote(x.at[c, i], x.at[c, i], ag_send.at[0], ag_recv.at[d2 * 4 + d1, 0], sibling).wait_recv()

    def event(d1, d2):
        if (d1, d2) != (0, 0):
            arrive(d1, d2)
        if d2 == 0:
            if d1 == 0:
                whole(0, 0, 1, 0, right1, 16)
                whole(0, 0, 3, 0, left1, 17)
            elif d1 == 1:
                pair(1, 0, 2, 0, right1, 18, 0)
            elif d1 == 3:
                pair(3, 0, 2, 0, left1, 19, 1)
            whole(d1, 0, d1, 1, right2, d1)
            whole(d1, 0, d1, 3, left2, 4 + d1)
        elif d2 == 1:
            pair(d1, 1, d1, 2, right2, 8 + d1, 0)
        elif d2 == 3:
            pair(d1, 3, d1, 2, left2, 12 + d1, 1)
        i = spot(d1, d2)
        copy = remote(x.at[c, i], x.at[c, i], core_send.at[d2 * 4 + d1], core_recv.at[d2 * 4 + d1], sibling)
        copy.start()
        sent.append((core_send, d2 * 4 + d1, 4))

    def from_sibling(d2):
        for d1 in range(4):
            i = ((p1 + 4 - d2) % SIDE) * SIDE + (p2 + 4 - d1) % SIDE
            part = x.at[1 - c, i]
            remote(part, part, core_send.at[0], core_recv.at[d2 * 4 + d1], sibling).wait_recv()

    events = {
        0: [(0, 0), (1, 0), (3, 0), (0, 1), (0, 3), (2, 0)],
        1: [(1, 1), (1, 3)],
        2: [(3, 1), (3, 3)],
        3: [(2, 1), (2, 3)],
        6: [(0, 2)],
        8: [(1, 2)],
        10: [(3, 2)],
        12: [(2, 2)],
    }
    sibling_groups = {2: 0, 6: 1, 10: 3, 14: 2}

    @pl.loop(0, 16)
    def _(u):
        for when in range(16):
            if when in events or when in sibling_groups or when in (0, 2):
                @pl.when(u == when)
                def _(when=when):
                    for d1, d2 in events.get(when, ()):
                        event(d1, d2)
                    if when in (0, 2):
                        for k in range(4):
                            for n in range(2):
                                weights_in(4 * ((c + when // 2) % 2) + k, n).wait()
                    if when in sibling_groups:
                        from_sibling(sibling_groups[when])
        turn = u // 4
        d2 = turn + turn // 2 - 2 * (turn // 3)
        which = (u // 2) % 2
        half = (c + which) % 2
        base = (((1 - which) * p2 + which * p1 + 4 - d2) % SIDE) * SIDE

        @pl.loop(0, 2)
        def _(kk):
            k = (u % 2) * 2 + kk
            rows = x[half, pl.ds(base, SIDE), k].reshape(SIDE * ROWS, WIDE)
            part = jnp.dot(rows, w_in[half * 4 + k], preferred_element_type=f32)
            part = part.reshape(SIDE, ROWS, 2 * f)

            @pl.when(k == 0)
            def _():
                acc[which, pl.ds(base, SIDE)] = part

            @pl.when(k > 0)
            def _():
                acc[which, pl.ds(base, SIDE)] += part

    @pl.loop(0, 16)
    def _(i):
        flip = (i % SIDE) * SIDE + i // SIDE
        total = acc[0, i] + acc[1, flip]
        gated = total[:, :f]
        value = (gated / (1.0 + jnp.exp(-gated)) * total[:, f:]).astype(jnp.bfloat16)
        hid[0, i] = value
        hid[1, flip] = value

    for sems, slot, size in sent:
        part = x.at[c, 0, pl.ds(0, size)]
        remote(part, part, sems.at[slot], ag_recv.at[0, 0], sibling).wait_send()
    for o in range(8):
        weights_out(o).wait()

    def block(own, d, s):
        return (own + 3 - s) % SIDE if d == 0 else (own + 1 + s) % SIDE

    def q_copy(s, d, jj):
        i = block(p1, d, s) * SIDE + block(p2, d, jj)
        return remote(x.at[1 - c, i, pl.ds(2 * d, 2)], q.at[s, d, jj], q_send.at[s * 8 + d * 4 + jj],
                      q_recv.at[s * 8 + d * 4 + jj], sibling)

    def r1_copy(s, d, jj):
        i = block(p2, d, s) * SIDE + block(p1, d, jj)
        return remote(x.at[c, i, pl.ds(2 * d, 2)], r1.at[s, d, jj], r1_send.at[s * 8 + d * 4 + jj],
                      r1_recv.at[s * 8 + d * 4 + jj], left2 if d else right2)

    def r2_copy(d, jj):
        i = p2 * SIDE + block(p1, d, jj)
        return remote(x.at[c, i, pl.ds(2 * d, 2)], r2.at[jj, d], r2_send.at[jj * 2 + d],
                      r2_recv.at[jj * 2 + d], left1 if d else right1)

    for s in range(4):
        for which in (1, 0):
            half = (c + which) % 2
            own2 = p1 if which else p2
            for d in range(2):
                base = block(own2, d, s) * SIDE

                @pl.loop(0, 2)
                def _(kk):
                    k = 2 * d + kk
                    rows = hid[which, pl.ds(base, SIDE)].reshape(SIDE * ROWS, f)
                    part = jnp.dot(rows, w_out[half * 4 + k], preferred_element_type=f32)
                    x[half, pl.ds(base, SIDE), k] = part.astype(jnp.bfloat16).reshape(SIDE, ROWS, WIDE)

                if which:
                    @pl.loop(0, 4)
                    def _(jj):
                        q_copy(s, d, jj).start()

        def turn(jj):
            for d in range(2):
                i = block(p2, d, s) * SIDE + block(p1, d, jj)
                q_copy(s, d, jj).wait_recv()
                if s > 0:
                    r1_copy(s - 1, d, jj).wait_recv()
                if s == 3 and jj > 0:
                    r2_copy(d, jj - 1).wait_recv()
                for kk in range(2):
                    k = 2 * d + kk
                    total = x[c, i, k].astype(f32) + q[s, d, jj, kk].astype(f32)
                    if s > 0:
                        total = total + r1[s - 1, d, jj, kk].astype(f32)
                    if s == 3 and jj > 0:
                        total = total + r2[jj - 1, d, kk].astype(f32)
                    if s == 3 and jj == 3:
                        done[4 * c + k] = total.astype(jnp.bfloat16)
                    else:
                        x[c, i, k] = total.astype(jnp.bfloat16)
                if s < 3:
                    r1_copy(s, d, jj).start()
                elif jj < 3:
                    r2_copy(d, jj).start()

        if s < 3:
            pl.loop(0, 4)(turn)
        else:
            for jj in range(4):
                turn(jj)

    mine = done.at[pl.ds(4 * c, 4)]
    last = remote(mine, mine, done_sem.at[0], done_sem.at[1], sibling)
    last.start()
    for s in range(4):
        @pl.loop(0, 4)
        def _(jj):
            for d in range(2):
                q_copy(s, d, jj).wait_send()
                if s < 3:
                    r1_copy(s, d, jj).wait_send()
    for jj in range(3):
        for d in range(2):
            r2_copy(d, jj).wait_send()
    last.wait_send()
    other = done.at[pl.ds(4 * (1 - c), 4)]
    remote(other, other, done_sem.at[0], done_sem.at[1], sibling).wait_recv()
    out_ref[...] = done[...]


def experts_layer(rows, w_gate, w_up, w_down):
    f = w_gate.shape[2]
    bf16, f32 = jnp.bfloat16, jnp.float32
    dma = pltpu.SemaphoreType.DMA
    any_spec = pl.BlockSpec(memory_space=pl.ANY)
    vmem_spec = pl.BlockSpec(memory_space=pltpu.VMEM)
    return pl.pallas_call(
        expert_kernel,
        out_shape=jax.ShapeDtypeStruct((8, ROWS, WIDE), bf16),
        in_specs=[vmem_spec, any_spec, any_spec, any_spec],
        out_specs=vmem_spec,
        scratch_shapes=[
            pltpu.VMEM((2, 16, 4, ROWS, WIDE), bf16),
            pltpu.VMEM((8, WIDE, 2 * f), bf16),
            pltpu.VMEM((8, f, WIDE), bf16),
            pltpu.VMEM((2, 16, ROWS, 2 * f), f32),
            pltpu.VMEM((2, 16, ROWS, f), bf16),
            pltpu.VMEM((4, ROWS, WIDE), bf16),
            pltpu.VMEM((4, 2, 4, 2, ROWS, WIDE), bf16),
            pltpu.VMEM((3, 2, 4, 2, ROWS, WIDE), bf16),
            pltpu.VMEM((3, 2, 2, ROWS, WIDE), bf16),
            pltpu.VMEM((8, ROWS, WIDE), bf16),
            dma((3, 8)), dma((2,)), dma((20,)), dma((16, 2)), dma((16,)), dma((16,)),
            dma((32,)), dma((32,)), dma((24,)), dma((24,)), dma((6,)), dma((6,)), dma((2,)),
        ],
        compiler_params=pltpu.CompilerParams(
            collective_id=0, has_side_effects=True, vmem_limit_bytes=VMEM_LIMIT),
        cost_estimate=pl.CostEstimate(flops=2 * 768 * 8192 * 384 * 3, bytes_accessed=20_000_000, transcendentals=300_000),
    )(rows, w_gate, w_up, w_down)


def on_device(
    inner,
    gate_in,
    w_low,
    w_state,
    w_dt,
    dt_bias,
    decay_rate,
    skip_gain,
    w_router,
    expert_ids,
    w_gate,
    w_up,
    w_down,
):
    tokens, channels = inner.shape
    experts = lax.axis_size("exp")
    rank_part = jnp.dot(inner, w_low, preferred_element_type=jnp.float32)
    state_part = jnp.dot(inner, w_state, preferred_element_type=jnp.float32)
    rank_sum, state_sum = lax.psum((rank_part, state_part), "exp")
    mixer_out, logits_part = mixer(
        rank_sum, state_sum, inner, gate_in, w_dt, dt_bias, decay_rate, skip_gain, w_router
    )
    logits = lax.psum(logits_part, "exp")
    catalog = jnp.arange(NE, dtype=jnp.int32)
    chosen = jnp.sum(
        jnp.where(expert_ids[:, :, None] == catalog[None, None, :], logits[:, None, :], 0.0), axis=2
    )
    shares = 1.0 / (1.0 + jnp.exp(chosen[:, ::-1] - chosen))
    window = jnp.arange(experts, dtype=jnp.int32)
    hit_table = (expert_ids[:, :, None] == window[None, None, :]).astype(jnp.int32)
    load_count = jnp.sum(hit_table, axis=1)
    earlier = jnp.cumsum(load_count, axis=0) - load_count
    slot_index = jnp.sum(hit_table * earlier[:, None, :], axis=2)
    matches = (slot_index[:, :, None] == jnp.arange(CAP, dtype=jnp.int32)[None, None, :]).astype(
        jnp.float32
    )
    picked = hit_table.astype(jnp.float32)
    selector = jnp.einsum("tke,tkc->ect", picked, matches).astype(jnp.bfloat16)
    outgoing = jnp.einsum(
        "ect,td->ecd", selector, mixer_out, preferred_element_type=jnp.float32
    ).astype(jnp.bfloat16)
    arrived = lax.all_to_all(outgoing, "exp", split_axis=0, concat_axis=2, tiled=True)[0]
    core = lax.axis_index("seq") % 2
    pieces = arrived.reshape(CAP, 8, WIDE).transpose(1, 0, 2)
    both = jnp.concatenate([jnp.where(core == 0, pieces, 0), jnp.where(core == 1, pieces, 0)], axis=1)
    summed = experts_layer(both, w_gate, w_up, w_down)
    summed = lax.dynamic_slice_in_dim(summed, core * CAP, CAP, axis=1)
    returned = lax.all_to_all(summed.reshape(experts, 2, CAP, WIDE), "exp", split_axis=0, concat_axis=0, tiled=True)
    returned = returned.transpose(0, 2, 1, 3)
    weighting = jnp.einsum(
        "tk,tke,tkc->tec", shares, picked, matches, precision=lax.Precision.HIGHEST
    )
    combined = jnp.dot(
        weighting.reshape(tokens, experts * CAP),
        returned.reshape(experts * CAP, channels).astype(jnp.float32),
        precision=lax.Precision.HIGHEST,
    )
    return mixer_out.astype(jnp.float32) + combined


def solution(mesh):
    in_specs = (
        P("seq", "exp"),
        P("seq", "exp"),
        P("exp", None),
        P("exp", None),
        P(None, "exp"),
        P("exp"),
        P("exp", None),
        P("exp"),
        P("exp", None),
        P("seq", None),
        P("exp", None, "seq"),
        P("exp", None, "seq"),
        P("exp", "seq", None),
    )
    out_specs = P("seq", "exp")
    return jax.shard_map(
        on_device, mesh=mesh, in_specs=in_specs, out_specs=out_specs, check_vma=False
    )
```

```python
import functools

import jax
import jax.numpy as jnp
from jax import lax
from jax.experimental import pallas as pl
from jax.experimental.pallas import tpu as pltpu
from jax.sharding import PartitionSpec as P

N = 16
NE = 16
CAP = 24
LANES = 128
LOG2E = 1.4426950408889634
VMEM_LIMIT = 60 * 1024 * 1024


def softplus(v):
    return jnp.maximum(v, 0.0) + jnp.log1p(jnp.exp(-jnp.abs(v)))


def spread(ref, cols):
    tokens = cols.shape[0]
    for n in range(N):
        ref[pl.ds(n, tokens, stride=N), :] = jnp.broadcast_to(
            cols[:, n : n + 1], (tokens, LANES)
        )

def mixer_kernel(inner_ref, wlow_ref, wstate_ref, bias_ref, rate_ref, skip_ref, wr_ref, wdt_hbm, gate_hbm,
                 mixer_ref, logits_ref,
                 wdt, gate_s, low_part, state_part, low_send, low_got, state_got, low_all, state_all,
                 dt_s, u_s, y_s, b_s, c_s, ends, heard, carries, h0,
                 load_sem, low_sem, state_sem, low_sem2, state_sem2, end_sem, carry_sem):
    tokens, channels = inner_ref.shape
    tiles = channels // LANES
    count, experts = lax.axis_size("seq"), lax.axis_size("exp")
    seq, z = lax.axis_index("seq"), lax.axis_index("exp")
    chunk = tokens // experts
    f32, bf16 = jnp.float32, jnp.bfloat16
    mesh_ids = pl.DeviceIdType.MESH

    load_dt = pltpu.make_async_copy(wdt_hbm, wdt, load_sem.at[0])
    load_gate = pltpu.make_async_copy(gate_hbm, gate_s, load_sem.at[1])
    load_dt.start()
    load_gate.start()

    barrier = pltpu.get_barrier_semaphore()
    for k in range(1, experts):
        pl.semaphore_signal(barrier, inc=1, device_id={"exp": (z + k) % experts}, device_id_type=mesh_ids)

    @pl.loop(1, count)
    def _(k):
        pl.semaphore_signal(barrier, inc=1, device_id={"seq": (seq + k) % count}, device_id_type=mesh_ids)

    def remote(src, dst, send, recv, device):
        return pltpu.make_async_remote_copy(
            src_ref=src, dst_ref=dst, send_sem=send, recv_sem=recv, device_id=device, device_id_type=mesh_ids)

    values = inner_ref[...]
    low = jnp.dot(values, wlow_ref[...], preferred_element_type=f32)
    low_part[...] = low.reshape(low_part.shape)
    low_send[...] = low.astype(bf16).reshape(low_send.shape)
    state = jnp.dot(values, wstate_ref[...], preferred_element_type=f32)
    state_part[:, :, : 2 * N] = state.reshape(experts, chunk, 2 * N)
    state_part[:, :, 2 * N :] = jnp.zeros((experts, chunk, LANES - 2 * N), f32)
    pl.semaphore_wait(barrier, experts - 1 + count - 1)
    first = []
    for k in range(1, experts):
        to = (z + k) % experts
        first.append(remote(low_send.at[to], low_got.at[k - 1], low_sem.at[0, k], low_sem.at[1, k], {"exp": to}))
        first.append(remote(state_part.at[to], state_got.at[k - 1], state_sem.at[0, k], state_sem.at[1, k], {"exp": to}))
    for copy in first:
        copy.start()
    for copy in first:
        copy.wait_recv()
    low_sum, state_sum = low_part[z], state_part[z]
    for k in range(1, experts):
        low_sum = low_sum + low_got[k - 1].astype(f32)
        state_sum = state_sum + state_got[k - 1]
    low_all[z] = low_sum.astype(bf16)
    state_all[z] = state_sum
    second = []
    for k in range(1, experts):
        to = {"exp": (z + k) % experts}
        second.append(remote(low_all.at[z], low_all.at[z], low_sem2.at[0, k], low_sem2.at[1, k], to))
        second.append(remote(state_all.at[z], state_all.at[z], state_sem2.at[0, k], state_sem2.at[1, k], to))
    for copy in second:
        copy.start()
    for copy in second:
        copy.wait_recv()

    load_dt.wait()
    low_b = low_all[...].reshape(tokens, low_all.shape[2])
    for j in range(channels // 256):
        cols = pl.ds(j * 256, 256)
        dt = softplus(jnp.dot(low_b, wdt[:, cols], preferred_element_type=f32) + bias_ref[:, cols])
        u = dt * inner_ref[:, cols].astype(f32)
        for k in range(2):
            part = slice(k * LANES, (k + 1) * LANES)
            dt_s[pl.ds(2 * j + k, tokens, stride=tiles), :] = dt[:, part]
            u_s[pl.ds(2 * j + k, tokens, stride=tiles), :] = u[:, part]
    maps = state_all[...].reshape(tokens, LANES)
    spread(b_s, maps[:, :N])
    for half in range(2):
        rate = [rate_ref[n, half * 8 : half * 8 + 8, :] for n in range(N)]

        def step(t, carry):
            total, h = carry
            at = pl.multiple_of(t * tiles + half * 8, 8)
            dt = dt_s[pl.ds(at, 8), :]
            u = u_s[pl.ds(at, 8), :]
            new = []
            for n in range(N):
                b = b_s[pl.ds(t * N + n, 1), :]
                new.append(jnp.exp2(dt * rate[n]) * h[n] + u * b)
            return total + dt, tuple(new)

        zero = jnp.zeros((8, LANES), f32)
        total, h = lax.fori_loop(0, tokens, step, (zero, (zero,) * N), unroll=4)
        for n in range(N):
            ends[2 * n + half, 0] = jnp.exp2(total * rate[n])
            ends[2 * n + half, 1] = h[n]

    @pl.loop(1, count)
    def _(k):
        to = (seq + k) % count
        remote(ends.at[to], heard.at[seq], end_sem.at[0], end_sem.at[1], {"seq": to}).start()

    heard[seq] = ends[seq]
    spread(c_s, maps[:, N : 2 * N])
    others = pl.ds(0, count - 1)
    remote(ends.at[others], heard.at[others], end_sem.at[0], end_sem.at[1], {"seq": (seq + 1) % count}).wait()

    def join(s, carry):
        carries[s] = carry
        return heard[s, 0] * carry + heard[s, 1]

    lax.fori_loop(0, count, join, jnp.zeros((8, LANES), f32), unroll=4)

    @pl.loop(1, count)
    def _(k):
        to = (seq + k) % count
        remote(carries.at[to], h0.at[seq], carry_sem.at[0], carry_sem.at[1], {"seq": to}).start()

    h0[seq] = carries[seq]
    remote(carries.at[others], h0.at[others], carry_sem.at[0], carry_sem.at[1], {"seq": (seq + 1) % count}).wait()

    for half in range(2):
        rate = [rate_ref[n, half * 8 : half * 8 + 8, :] for n in range(N)]

        def step(t, h):
            at = pl.multiple_of(t * tiles + half * 8, 8)
            dt = dt_s[pl.ds(at, 8), :]
            u = u_s[pl.ds(at, 8), :]
            new = []
            y = None
            for n in range(N):
                b = b_s[pl.ds(t * N + n, 1), :]
                c = c_s[pl.ds(t * N + n, 1), :]
                new.append(jnp.exp2(dt * rate[n]) * h[n] + u * b)
                y = new[n] * c if y is None else y + new[n] * c
            y_s[pl.ds(at, 8), :] = y
            return tuple(new)

        lax.fori_loop(0, tokens, step, tuple(h0[2 * n + half] for n in range(N)), unroll=4)
    load_gate.wait()
    for j in range(tiles):
        cols = pl.ds(j * LANES, LANES)
        y = y_s[pl.ds(j, tokens, stride=tiles), :]
        gate = gate_s[:, cols].astype(f32)
        value = (y + skip_ref[:, cols] * inner_ref[:, cols].astype(f32)) * (gate / (1.0 + jnp.exp(-gate)))
        mixer_ref[:, cols] = value.astype(bf16)
    logits_ref[...] = jnp.dot(mixer_ref[...], wr_ref[...], preferred_element_type=f32)
    for copy in first + second:
        copy.wait_send()


def mixer(inner, gate_in, w_low, w_state, w_dt, dt_bias, decay_rate, skip_gain, w_router):
    tokens, channels = inner.shape
    rank = w_low.shape[1]
    tiles = channels // LANES
    count, experts = lax.axis_size("seq"), lax.axis_size("exp")
    chunk = tokens // experts
    f32, bf16 = jnp.float32, jnp.bfloat16
    rate = (decay_rate * -LOG2E).T.reshape(N, tiles, LANES)
    dma = pltpu.SemaphoreType.DMA
    any_spec = pl.BlockSpec(memory_space=pl.ANY)
    vmem_spec = pl.BlockSpec(memory_space=pltpu.VMEM)
    return pl.pallas_call(
        mixer_kernel,
        out_shape=(
            jax.ShapeDtypeStruct((tokens, channels), bf16),
            jax.ShapeDtypeStruct((tokens, NE), f32),
        ),
        in_specs=[vmem_spec] * 7 + [any_spec] * 2,
        out_specs=(vmem_spec, vmem_spec),
        scratch_shapes=[
            pltpu.VMEM(w_dt.shape, bf16),
            pltpu.VMEM((tokens, channels), bf16),
            pltpu.VMEM((experts, chunk, rank), f32),
            pltpu.VMEM((experts, chunk, LANES), f32),
            pltpu.VMEM((experts, chunk, rank), bf16),
            pltpu.VMEM((experts - 1, chunk, rank), bf16),
            pltpu.VMEM((experts - 1, chunk, LANES), f32),
            pltpu.VMEM((experts, chunk, rank), bf16),
            pltpu.VMEM((experts, chunk, LANES), f32),
        ]
        + [pltpu.VMEM((tokens * tiles, LANES), f32)] * 3
        + [pltpu.VMEM((tokens * N, LANES), f32)] * 2
        + [pltpu.VMEM((count, 2, 8, LANES), f32)] * 2
        + [pltpu.VMEM((count, 8, LANES), f32)] * 2
        + [dma((2,))] + [dma((2, experts))] * 4 + [dma((2,))] * 2,
        compiler_params=pltpu.CompilerParams(
            collective_id=1, has_side_effects=True, vmem_limit_bytes=VMEM_LIMIT),
    )(inner, w_low, w_state, dt_bias[None], rate, skip_gain[None], w_router, w_dt, gate_in)


ROWS = 2 * CAP
WIDE = 1024
SIDE = 4


def expert_kernel(rows_ref, gate_ref, up_ref, down_ref, out_ref,
                  x, w_in, w_out, acc, hid, first, q, r1, r2, done,
                  w_sem, first_sem, ag_send, ag_recv, core_send, core_recv,
                  q_send, q_recv, r1_send, r1_recv, r2_send, r2_recv, done_sem):
    seq = lax.axis_index("seq")
    c = seq % 2
    chip = seq // 2
    f = w_out.shape[1]
    f32 = jnp.float32
    p1 = (1 - c) * (chip % SIDE) + c * (chip // SIDE)
    p2 = (1 - c) * (chip // SIDE) + c * (chip % SIDE)
    me = p2 * SIDE + p1

    def at(i1, i2, core=None):
        where = (1 - c) * (i2 * SIDE + i1) + c * (i1 * SIDE + i2)
        return {"seq": where * 2 + (c if core is None else core)}

    sibling = at(p1, p2, 1 - c)
    right1, left1 = at((p1 + 1) % SIDE, p2), at((p1 + 3) % SIDE, p2)
    right2, left2 = at(p1, (p2 + 1) % SIDE), at(p1, (p2 + 3) % SIDE)

    def remote(src, dst, send, recv, device):
        return pltpu.make_async_remote_copy(
            src_ref=src, dst_ref=dst, send_sem=send, recv_sem=recv,
            device_id=device, device_id_type=pl.DeviceIdType.MESH)

    def weights_in(o, n):
        return pltpu.make_async_copy(
            (gate_ref, up_ref)[n].at[0, pl.ds(o * WIDE, WIDE), :], w_in.at[o, :, pl.ds(n * f, f)], w_sem.at[n, o])

    def weights_out(o):
        return pltpu.make_async_copy(down_ref.at[0, :, pl.ds(o * WIDE, WIDE)], w_out.at[o], w_sem.at[2, o])

    for o in range(8):
        for n in range(2):
            weights_in((4 * c + o) % 8, n).start()
    for o in range(8):
        weights_out(o).start()

    barrier = pltpu.get_barrier_semaphore()
    for peer in (sibling, right1, left1, right2, left2):
        pl.semaphore_signal(barrier, inc=1, device_id=peer, device_id_type=pl.DeviceIdType.MESH)
    pl.semaphore_wait(barrier, 5)

    swap = remote(rows_ref.at[pl.ds(4 * (1 - c), 4)], first, first_sem.at[0], first_sem.at[1], sibling)
    swap.start()
    swap.wait()
    for k in range(4):
        x[c, me, k] = rows_ref[4 * c + k] + first[k]

    sent = []

    def spot(d1, d2):
        return ((p2 + 4 - d2) % SIDE) * SIDE + (p1 + 4 - d1) % SIDE

    def whole(d1, d2, n1, n2, device, slot):
        i = spot(d1, d2)
        copy = remote(x.at[c, i], x.at[c, i], ag_send.at[slot], ag_recv.at[n2 * 4 + n1, 0], device)
        copy.start()
        sent.append((ag_send, slot, 4))

    def pair(d1, d2, n1, n2, device, slot, k):
        i = spot(d1, d2)
        part = x.at[c, i, pl.ds(2 * k, 2)]
        copy = remote(part, part, ag_send.at[slot], ag_recv.at[n2 * 4 + n1, k], device)
        copy.start()
        sent.append((ag_send, slot, 2))

    def arrive(d1, d2):
        i = spot(d1, d2)
        if d2 == 2 or (d2 == 0 and d1 == 2):
            for k in range(2):
                part = x.at[c, i, pl.ds(2 * k, 2)]
                remote(part, part, ag_send.at[0], ag_recv.at[d2 * 4 + d1, k], sibling).wait_recv()
        else:
            remote(x.at[c, i], x.at[c, i], ag_send.at[0], ag_recv.at[d2 * 4 + d1, 0], sibling).wait_recv()

    def event(d1, d2):
        if (d1, d2) != (0, 0):
            arrive(d1, d2)
        if d2 == 0:
            if d1 == 0:
                whole(0, 0, 1, 0, right1, 16)
                whole(0, 0, 3, 0, left1, 17)
            elif d1 == 1:
                pair(1, 0, 2, 0, right1, 18, 0)
            elif d1 == 3:
                pair(3, 0, 2, 0, left1, 19, 1)
            whole(d1, 0, d1, 1, right2, d1)
            whole(d1, 0, d1, 3, left2, 4 + d1)
        elif d2 == 1:
            pair(d1, 1, d1, 2, right2, 8 + d1, 0)
        elif d2 == 3:
            pair(d1, 3, d1, 2, left2, 12 + d1, 1)
        i = spot(d1, d2)
        copy = remote(x.at[c, i], x.at[c, i], core_send.at[d2 * 4 + d1], core_recv.at[d2 * 4 + d1], sibling)
        copy.start()
        sent.append((core_send, d2 * 4 + d1, 4))

    def from_sibling(d2):
        for d1 in range(4):
            i = ((p1 + 4 - d2) % SIDE) * SIDE + (p2 + 4 - d1) % SIDE
            part = x.at[1 - c, i]
            remote(part, part, core_send.at[0], core_recv.at[d2 * 4 + d1], sibling).wait_recv()

    events = {
        0: [(0, 0), (1, 0), (3, 0), (0, 1), (0, 3), (2, 0)],
        1: [(1, 1), (1, 3)],
        2: [(3, 1), (3, 3)],
        3: [(2, 1), (2, 3)],
        6: [(0, 2)],
        8: [(1, 2)],
        10: [(3, 2)],
        12: [(2, 2)],
    }
    sibling_groups = {2: 0, 6: 1, 10: 3, 14: 2}

    @pl.loop(0, 16)
    def _(u):
        for when in range(16):
            if when in events or when in sibling_groups or when in (0, 2):
                @pl.when(u == when)
                def _(when=when):
                    for d1, d2 in events.get(when, ()):
                        event(d1, d2)
                    if when in (0, 2):
                        for k in range(4):
                            for n in range(2):
                                weights_in(4 * ((c + when // 2) % 2) + k, n).wait()
                    if when in sibling_groups:
                        from_sibling(sibling_groups[when])
        turn = u // 4
        d2 = turn + turn // 2 - 2 * (turn // 3)
        which = (u // 2) % 2
        half = (c + which) % 2
        base = (((1 - which) * p2 + which * p1 + 4 - d2) % SIDE) * SIDE

        @pl.loop(0, 2)
        def _(kk):
            k = (u % 2) * 2 + kk
            rows = x[half, pl.ds(base, SIDE), k].reshape(SIDE * ROWS, WIDE)
            part = jnp.dot(rows, w_in[half * 4 + k], preferred_element_type=f32)
            part = part.reshape(SIDE, ROWS, 2 * f)

            @pl.when(k == 0)
            def _():
                acc[which, pl.ds(base, SIDE)] = part

            @pl.when(k > 0)
            def _():
                acc[which, pl.ds(base, SIDE)] += part

    @pl.loop(0, 16)
    def _(i):
        flip = (i % SIDE) * SIDE + i // SIDE
        total = acc[0, i] + acc[1, flip]
        gated = total[:, :f]
        value = (gated / (1.0 + jnp.exp(-gated)) * total[:, f:]).astype(jnp.bfloat16)
        hid[0, i] = value
        hid[1, flip] = value

    for sems, slot, size in sent:
        part = x.at[c, 0, pl.ds(0, size)]
        remote(part, part, sems.at[slot], ag_recv.at[0, 0], sibling).wait_send()
    for o in range(8):
        weights_out(o).wait()

    def block(own, d, s):
        return (own + 3 - s) % SIDE if d == 0 else (own + 1 + s) % SIDE

    def q_copy(s, d, jj):
        i = block(p1, d, s) * SIDE + block(p2, d, jj)
        return remote(x.at[1 - c, i, pl.ds(2 * d, 2)], q.at[s, d, jj], q_send.at[s * 8 + d * 4 + jj],
                      q_recv.at[s * 8 + d * 4 + jj], sibling)

    def r1_copy(s, d, jj):
        i = block(p2, d, s) * SIDE + block(p1, d, jj)
        return remote(x.at[c, i, pl.ds(2 * d, 2)], r1.at[s, d, jj], r1_send.at[s * 8 + d * 4 + jj],
                      r1_recv.at[s * 8 + d * 4 + jj], left2 if d else right2)

    def r2_copy(d, jj):
        i = p2 * SIDE + block(p1, d, jj)
        return remote(x.at[c, i, pl.ds(2 * d, 2)], r2.at[jj, d], r2_send.at[jj * 2 + d],
                      r2_recv.at[jj * 2 + d], left1 if d else right1)

    for s in range(4):
        for which in (1, 0):
            half = (c + which) % 2
            own2 = p1 if which else p2
            for d in range(2):
                base = block(own2, d, s) * SIDE

                @pl.loop(0, 2)
                def _(kk):
                    k = 2 * d + kk
                    rows = hid[which, pl.ds(base, SIDE)].reshape(SIDE * ROWS, f)
                    part = jnp.dot(rows, w_out[half * 4 + k], preferred_element_type=f32)
                    x[half, pl.ds(base, SIDE), k] = part.astype(jnp.bfloat16).reshape(SIDE, ROWS, WIDE)

                if which:
                    @pl.loop(0, 4)
                    def _(jj):
                        q_copy(s, d, jj).start()

        def turn(jj):
            for d in range(2):
                i = block(p2, d, s) * SIDE + block(p1, d, jj)
                q_copy(s, d, jj).wait_recv()
                if s > 0:
                    r1_copy(s - 1, d, jj).wait_recv()
                if s == 3 and jj > 0:
                    r2_copy(d, jj - 1).wait_recv()
                for kk in range(2):
                    k = 2 * d + kk
                    total = x[c, i, k].astype(f32) + q[s, d, jj, kk].astype(f32)
                    if s > 0:
                        total = total + r1[s - 1, d, jj, kk].astype(f32)
                    if s == 3 and jj > 0:
                        total = total + r2[jj - 1, d, kk].astype(f32)
                    if s == 3 and jj == 3:
                        done[4 * c + k] = total.astype(jnp.bfloat16)
                    else:
                        x[c, i, k] = total.astype(jnp.bfloat16)
                if s < 3:
                    r1_copy(s, d, jj).start()
                elif jj < 3:
                    r2_copy(d, jj).start()

        if s < 3:
            pl.loop(0, 4)(turn)
        else:
            for jj in range(4):
                turn(jj)

    mine = done.at[pl.ds(4 * c, 4)]
    last = remote(mine, mine, done_sem.at[0], done_sem.at[1], sibling)
    last.start()
    for s in range(4):
        @pl.loop(0, 4)
        def _(jj):
            for d in range(2):
                q_copy(s, d, jj).wait_send()
                if s < 3:
                    r1_copy(s, d, jj).wait_send()
    for jj in range(3):
        for d in range(2):
            r2_copy(d, jj).wait_send()
    last.wait_send()
    other = done.at[pl.ds(4 * (1 - c), 4)]
    remote(other, other, done_sem.at[0], done_sem.at[1], sibling).wait_recv()
    out_ref[...] = done[...]


def experts_layer(rows, w_gate, w_up, w_down):
    f = w_gate.shape[2]
    bf16, f32 = jnp.bfloat16, jnp.float32
    dma = pltpu.SemaphoreType.DMA
    any_spec = pl.BlockSpec(memory_space=pl.ANY)
    vmem_spec = pl.BlockSpec(memory_space=pltpu.VMEM)
    return pl.pallas_call(
        expert_kernel,
        out_shape=jax.ShapeDtypeStruct((8, ROWS, WIDE), bf16),
        in_specs=[vmem_spec, any_spec, any_spec, any_spec],
        out_specs=vmem_spec,
        scratch_shapes=[
            pltpu.VMEM((2, 16, 4, ROWS, WIDE), bf16),
            pltpu.VMEM((8, WIDE, 2 * f), bf16),
            pltpu.VMEM((8, f, WIDE), bf16),
            pltpu.VMEM((2, 16, ROWS, 2 * f), f32),
            pltpu.VMEM((2, 16, ROWS, f), bf16),
            pltpu.VMEM((4, ROWS, WIDE), bf16),
            pltpu.VMEM((4, 2, 4, 2, ROWS, WIDE), bf16),
            pltpu.VMEM((3, 2, 4, 2, ROWS, WIDE), bf16),
            pltpu.VMEM((3, 2, 2, ROWS, WIDE), bf16),
            pltpu.VMEM((8, ROWS, WIDE), bf16),
            dma((3, 8)), dma((2,)), dma((20,)), dma((16, 2)), dma((16,)), dma((16,)),
            dma((32,)), dma((32,)), dma((24,)), dma((24,)), dma((6,)), dma((6,)), dma((2,)),
        ],
        compiler_params=pltpu.CompilerParams(
            collective_id=0, has_side_effects=True, vmem_limit_bytes=VMEM_LIMIT),
        cost_estimate=pl.CostEstimate(flops=2 * 768 * 8192 * 384 * 3, bytes_accessed=20_000_000, transcendentals=300_000),
    )(rows, w_gate, w_up, w_down)


def on_device(
    inner,
    gate_in,
    w_low,
    w_state,
    w_dt,
    dt_bias,
    decay_rate,
    skip_gain,
    w_router,
    expert_ids,
    w_gate,
    w_up,
    w_down,
):
    tokens, channels = inner.shape
    experts = lax.axis_size("exp")
    mixer_out, logits_part = mixer(
        inner, gate_in, w_low, w_state, w_dt, dt_bias, decay_rate, skip_gain, w_router
    )
    logits = lax.psum(logits_part, "exp")
    catalog = jnp.arange(NE, dtype=jnp.int32)
    chosen = jnp.sum(
        jnp.where(expert_ids[:, :, None] == catalog[None, None, :], logits[:, None, :], 0.0), axis=2
    )
    shares = 1.0 / (1.0 + jnp.exp(chosen[:, ::-1] - chosen))
    window = jnp.arange(experts, dtype=jnp.int32)
    hit_table = (expert_ids[:, :, None] == window[None, None, :]).astype(jnp.int32)
    load_count = jnp.sum(hit_table, axis=1)
    earlier = jnp.cumsum(load_count, axis=0) - load_count
    slot_index = jnp.sum(hit_table * earlier[:, None, :], axis=2)
    matches = (slot_index[:, :, None] == jnp.arange(CAP, dtype=jnp.int32)[None, None, :]).astype(
        jnp.float32
    )
    picked = hit_table.astype(jnp.float32)
    selector = jnp.einsum("tke,tkc->ect", picked, matches).astype(jnp.bfloat16)
    outgoing = jnp.einsum(
        "ect,td->ecd", selector, mixer_out, preferred_element_type=jnp.float32
    ).astype(jnp.bfloat16)
    arrived = lax.all_to_all(outgoing, "exp", split_axis=0, concat_axis=2, tiled=True)[0]
    core = lax.axis_index("seq") % 2
    pieces = arrived.reshape(CAP, 8, WIDE).transpose(1, 0, 2)
    both = jnp.concatenate([jnp.where(core == 0, pieces, 0), jnp.where(core == 1, pieces, 0)], axis=1)
    summed = experts_layer(both, w_gate, w_up, w_down)
    summed = lax.dynamic_slice_in_dim(summed, core * CAP, CAP, axis=1)
    returned = lax.all_to_all(summed.reshape(experts, 2, CAP, WIDE), "exp", split_axis=0, concat_axis=0, tiled=True)
    returned = returned.transpose(0, 2, 1, 3)
    weighting = jnp.einsum(
        "tk,tke,tkc->tec", shares, picked, matches, precision=lax.Precision.HIGHEST
    )
    combined = jnp.dot(
        weighting.reshape(tokens, experts * CAP),
        returned.reshape(experts * CAP, channels).astype(jnp.float32),
        precision=lax.Precision.HIGHEST,
    )
    return mixer_out.astype(jnp.float32) + combined


def solution(mesh):
    in_specs = (
        P("seq", "exp"),
        P("seq", "exp"),
        P("exp", None),
        P("exp", None),
        P(None, "exp"),
        P("exp"),
        P("exp", None),
        P("exp"),
        P("exp", None),
        P("seq", None),
        P("exp", None, "seq"),
        P("exp", None, "seq"),
        P("exp", "seq", None),
    )
    out_specs = P("seq", "exp")
    return jax.shard_map(
        on_device, mesh=mesh, in_specs=in_specs, out_specs=out_specs, check_vma=False
    )
```

```python
import functools

import jax
import jax.numpy as jnp
from jax import lax
from jax.experimental import pallas as pl
from jax.experimental.pallas import tpu as pltpu
from jax.sharding import PartitionSpec as P

N = 16
NE = 16
CAP = 24
LANES = 128
LOG2E = 1.4426950408889634
VMEM_LIMIT = 60 * 1024 * 1024


def softplus(v):
    return jnp.maximum(v, 0.0) + jnp.log1p(jnp.exp(-jnp.abs(v)))


def rows_dot(a, b):
    return lax.dot_general(a, b, (((1,), (1,)), ((), ())), preferred_element_type=jnp.float32)


def spread(ref, cols):
    tokens = cols.shape[0]
    for n in range(N):
        ref[pl.ds(n, tokens, stride=N), :] = jnp.broadcast_to(
            cols[:, n : n + 1], (tokens, LANES)
        )

def mixer_kernel(inner_ref, wlow_ref, wstate_ref, bias_ref, decay_ref, skip_ref, wr_ref, wdt_hbm, gate_hbm,
                 mixer_ref, logits_ref,
                 wdt, gate_s, low_part, state_part, low_send, low_got, state_got, low_all, state_all,
                 dt_s, u_s, y_s, b_s, c_s, rate_s, ends, heard, carries, h0,
                 load_sem, low_sem, state_sem, low_sem2, state_sem2, end_sem, carry_sem):
    tokens, channels = inner_ref.shape
    tiles = channels // LANES
    count, experts = lax.axis_size("seq"), lax.axis_size("exp")
    seq, z = lax.axis_index("seq"), lax.axis_index("exp")
    chunk = tokens // experts
    f32, bf16 = jnp.float32, jnp.bfloat16
    mesh_ids = pl.DeviceIdType.MESH

    load_dt = pltpu.make_async_copy(wdt_hbm, wdt, load_sem.at[0])
    load_gate = pltpu.make_async_copy(gate_hbm, gate_s, load_sem.at[1])
    load_dt.start()
    load_gate.start()

    barrier = pltpu.get_barrier_semaphore()
    for k in range(1, experts):
        pl.semaphore_signal(barrier, inc=1, device_id={"exp": (z + k) % experts}, device_id_type=mesh_ids)

    @pl.loop(1, count)
    def _(k):
        pl.semaphore_signal(barrier, inc=1, device_id={"seq": (seq + k) % count}, device_id_type=mesh_ids)

    def remote(src, dst, send, recv, device):
        return pltpu.make_async_remote_copy(
            src_ref=src, dst_ref=dst, send_sem=send, recv_sem=recv, device_id=device, device_id_type=mesh_ids)

    values = inner_ref[...]
    low = jnp.dot(values, wlow_ref[...], preferred_element_type=f32)
    low_part[...] = low.reshape(low_part.shape)
    low_send[...] = low.astype(bf16).reshape(low_send.shape)
    state = rows_dot(values, wstate_ref[...])
    state_part[:, :, : 2 * N] = state.reshape(experts, chunk, 2 * N)
    state_part[:, :, 2 * N :] = jnp.zeros((experts, chunk, LANES - 2 * N), f32)
    for j in range(tiles):
        rate_s[pl.ds(j, N, stride=tiles), :] = decay_ref[:, pl.ds(j * LANES, LANES)] * -LOG2E
    pl.semaphore_wait(barrier, experts - 1 + count - 1)
    first = []
    for k in range(1, experts):
        to = (z + k) % experts
        first.append(remote(low_send.at[to], low_got.at[k - 1], low_sem.at[0, k], low_sem.at[1, k], {"exp": to}))
        first.append(remote(state_part.at[to], state_got.at[k - 1], state_sem.at[0, k], state_sem.at[1, k], {"exp": to}))
    for copy in first:
        copy.start()
    for copy in first:
        copy.wait_recv()
    low_sum, state_sum = low_part[z], state_part[z]
    for k in range(1, experts):
        low_sum = low_sum + low_got[k - 1].astype(f32)
        state_sum = state_sum + state_got[k - 1]
    low_all[z] = low_sum.astype(bf16)
    state_all[z] = state_sum
    second = []
    for k in range(1, experts):
        to = {"exp": (z + k) % experts}
        second.append(remote(low_all.at[z], low_all.at[z], low_sem2.at[0, k], low_sem2.at[1, k], to))
        second.append(remote(state_all.at[z], state_all.at[z], state_sem2.at[0, k], state_sem2.at[1, k], to))
    for copy in second:
        copy.start()
    for copy in second:
        copy.wait_recv()

    load_dt.wait()
    low_b = low_all[...].reshape(tokens, low_all.shape[2])
    for j in range(channels // 256):
        cols = pl.ds(j * 256, 256)
        dt = softplus(jnp.dot(low_b, wdt[:, cols], preferred_element_type=f32) + bias_ref[:, cols])
        u = dt * inner_ref[:, cols].astype(f32)
        for k in range(2):
            part = slice(k * LANES, (k + 1) * LANES)
            dt_s[pl.ds(2 * j + k, tokens, stride=tiles), :] = dt[:, part]
            u_s[pl.ds(2 * j + k, tokens, stride=tiles), :] = u[:, part]
    maps = state_all[...].reshape(tokens, LANES)
    spread(b_s, maps[:, :N])
    for half in range(2):
        rate = [rate_s[pl.ds(n * tiles + half * 8, 8), :] for n in range(N)]

        def step(t, carry):
            total, h = carry
            at = pl.multiple_of(t * tiles + half * 8, 8)
            dt = dt_s[pl.ds(at, 8), :]
            u = u_s[pl.ds(at, 8), :]
            new = []
            for n in range(N):
                b = b_s[pl.ds(t * N + n, 1), :]
                new.append(jnp.exp2(dt * rate[n]) * h[n] + u * b)
            return total + dt, tuple(new)

        zero = jnp.zeros((8, LANES), f32)
        total, h = lax.fori_loop(0, tokens, step, (zero, (zero,) * N), unroll=4)
        for n in range(N):
            ends[2 * n + half, 0] = jnp.exp2(total * rate[n])
            ends[2 * n + half, 1] = h[n]

    @pl.loop(1, count)
    def _(k):
        to = (seq + k) % count
        remote(ends.at[to], heard.at[seq], end_sem.at[0], end_sem.at[1], {"seq": to}).start()

    heard[seq] = ends[seq]
    spread(c_s, maps[:, N : 2 * N])
    others = pl.ds(0, count - 1)
    remote(ends.at[others], heard.at[others], end_sem.at[0], end_sem.at[1], {"seq": (seq + 1) % count}).wait()

    def join(s, carry):
        carries[s] = carry
        return heard[s, 0] * carry + heard[s, 1]

    lax.fori_loop(0, count, join, jnp.zeros((8, LANES), f32), unroll=4)

    @pl.loop(1, count)
    def _(k):
        to = (seq + k) % count
        remote(carries.at[to], h0.at[seq], carry_sem.at[0], carry_sem.at[1], {"seq": to}).start()

    h0[seq] = carries[seq]
    remote(carries.at[others], h0.at[others], carry_sem.at[0], carry_sem.at[1], {"seq": (seq + 1) % count}).wait()

    for half in range(2):
        rate = [rate_s[pl.ds(n * tiles + half * 8, 8), :] for n in range(N)]

        def step(t, h):
            at = pl.multiple_of(t * tiles + half * 8, 8)
            dt = dt_s[pl.ds(at, 8), :]
            u = u_s[pl.ds(at, 8), :]
            new = []
            y = None
            for n in range(N):
                b = b_s[pl.ds(t * N + n, 1), :]
                c = c_s[pl.ds(t * N + n, 1), :]
                new.append(jnp.exp2(dt * rate[n]) * h[n] + u * b)
                y = new[n] * c if y is None else y + new[n] * c
            y_s[pl.ds(at, 8), :] = y
            return tuple(new)

        lax.fori_loop(0, tokens, step, tuple(h0[2 * n + half] for n in range(N)), unroll=4)
    load_gate.wait()
    for j in range(tiles):
        cols = pl.ds(j * LANES, LANES)
        y = y_s[pl.ds(j, tokens, stride=tiles), :]
        gate = gate_s[:, cols].astype(f32)
        value = (y + skip_ref[:, cols] * inner_ref[:, cols].astype(f32)) * (gate / (1.0 + jnp.exp(-gate)))
        mixer_ref[:, cols] = value.astype(bf16)
    logits_ref[...] = rows_dot(wr_ref[...], mixer_ref[...])
    for copy in first + second:
        copy.wait_send()


def mixer(inner, gate_in, w_low, w_state, w_dt, dt_bias, decay_rate, skip_gain, w_router):
    tokens, channels = inner.shape
    rank = w_low.shape[1]
    tiles = channels // LANES
    count, experts = lax.axis_size("seq"), lax.axis_size("exp")
    chunk = tokens // experts
    f32, bf16 = jnp.float32, jnp.bfloat16
    dma = pltpu.SemaphoreType.DMA
    any_spec = pl.BlockSpec(memory_space=pl.ANY)
    vmem_spec = pl.BlockSpec(memory_space=pltpu.VMEM)
    return pl.pallas_call(
        mixer_kernel,
        out_shape=(
            jax.ShapeDtypeStruct((tokens, channels), bf16),
            jax.ShapeDtypeStruct((NE, tokens), f32),
        ),
        in_specs=[vmem_spec] * 7 + [any_spec] * 2,
        out_specs=(vmem_spec, vmem_spec),
        scratch_shapes=[
            pltpu.VMEM(w_dt.shape, bf16),
            pltpu.VMEM((tokens, channels), bf16),
            pltpu.VMEM((experts, chunk, rank), f32),
            pltpu.VMEM((experts, chunk, LANES), f32),
            pltpu.VMEM((experts, chunk, rank), bf16),
            pltpu.VMEM((experts - 1, chunk, rank), bf16),
            pltpu.VMEM((experts - 1, chunk, LANES), f32),
            pltpu.VMEM((experts, chunk, rank), bf16),
            pltpu.VMEM((experts, chunk, LANES), f32),
        ]
        + [pltpu.VMEM((tokens * tiles, LANES), f32)] * 3
        + [pltpu.VMEM((tokens * N, LANES), f32)] * 2
        + [pltpu.VMEM((N * tiles, LANES), f32)]
        + [pltpu.VMEM((count, 2, 8, LANES), f32)] * 2
        + [pltpu.VMEM((count, 8, LANES), f32)] * 2
        + [dma((2,))] + [dma((2, experts))] * 4 + [dma((2,))] * 2,
        compiler_params=pltpu.CompilerParams(
            collective_id=1, has_side_effects=True, vmem_limit_bytes=VMEM_LIMIT),
    )(inner, w_low, w_state.T, dt_bias[None], decay_rate.T, skip_gain[None], w_router.T, w_dt, gate_in)


ROWS = 2 * CAP
WIDE = 1024
SIDE = 4


def expert_kernel(mixer_ref, logits_ref, ids_ref, gate_ref, up_ref, down_ref, out_ref,
                  x, w_in, w_out, acc, hid, swap_out, swap_in, picked, logits_got, q, r1, r2, done, back,
                  w_sem, swap_sem, hop_send, hop_recv, logit_sem, back_send, back_recv, pass_send, pass_recv, ag_send, ag_recv, core_send, core_recv,
                  q_send, q_recv, r1_send, r1_recv, r2_send, r2_recv):
    seq, z = lax.axis_index("seq"), lax.axis_index("exp")
    experts = lax.axis_size("exp")
    tokens = mixer_ref.shape[0]
    c = seq % 2
    chip = seq // 2
    holder = z // 2
    f = w_out.shape[1]
    f32 = jnp.float32
    p1 = (1 - c) * (chip % SIDE) + c * (chip // SIDE)
    p2 = (1 - c) * (chip // SIDE) + c * (chip % SIDE)
    me = p2 * SIDE + p1

    def at(i1, i2, core=None):
        where = (1 - c) * (i2 * SIDE + i1) + c * (i1 * SIDE + i2)
        return {"seq": where * 2 + (c if core is None else core)}

    sibling = at(p1, p2, 1 - c)
    right1, left1 = at((p1 + 1) % SIDE, p2), at((p1 + 3) % SIDE, p2)
    right2, left2 = at(p1, (p2 + 1) % SIDE), at(p1, (p2 + 3) % SIDE)

    def remote(src, dst, send, recv, device):
        return pltpu.make_async_remote_copy(
            src_ref=src, dst_ref=dst, send_sem=send, recv_sem=recv,
            device_id=device, device_id_type=pl.DeviceIdType.MESH)

    def weights_in(o, n):
        return pltpu.make_async_copy(
            (gate_ref, up_ref)[n].at[0, pl.ds(o * WIDE, WIDE), :], w_in.at[o, :, pl.ds(n * f, f)], w_sem.at[n, o])

    def weights_out(o):
        return pltpu.make_async_copy(down_ref.at[0, :, pl.ds(o * WIDE, WIDE)], w_out.at[o], w_sem.at[2, o])

    for o in range(8):
        for n in range(2):
            weights_in((4 * c + o) % 8, n).start()
    for o in range(8):
        weights_out(o).start()

    barrier = pltpu.get_barrier_semaphore()
    for peer in (sibling, right1, left1, right2, left2):
        pl.semaphore_signal(barrier, inc=1, device_id=peer, device_id_type=pl.DeviceIdType.MESH)
    for core in range(2):
        for k in range(1, experts):
            peer = {"seq": chip * 2 + core, "exp": (z + k) % experts}
            pl.semaphore_signal(barrier, inc=1, device_id=peer, device_id_type=pl.DeviceIdType.MESH)

    spots = (experts * ROWS, tokens)
    row = lax.broadcasted_iota(jnp.int32, spots, 0)
    one, none = jnp.ones(spots, jnp.int32), jnp.zeros(spots, jnp.int32)
    expert = none
    for e in range(1, experts):
        expert = expert + jnp.where(row >= e * ROWS, one, none)
    row = row - ROWS * expert
    core_of = jnp.where(row >= CAP, one, none)
    slot = row - CAP * core_of
    named0 = jnp.broadcast_to(ids_ref[0:1, :], spots) == expert
    named1 = jnp.broadcast_to(ids_ref[1:2, :], spots) == expert
    load = jnp.where(named0 | named1, 1.0, 0.0)
    before = jnp.where(
        lax.broadcasted_iota(jnp.int32, (tokens, tokens), 0) < lax.broadcasted_iota(jnp.int32, (tokens, tokens), 1),
        1.0, 0.0).astype(jnp.bfloat16)
    earlier = jnp.dot(load.astype(jnp.bfloat16), before, preferred_element_type=f32)
    fits = (earlier == slot.astype(f32)) & (core_of == c)
    taken = jnp.where(fits, load, 0.0).astype(jnp.bfloat16)

    def picks(side):
        cols = pl.ds(pl.multiple_of(side * WIDE, WIDE), WIDE)
        return jnp.dot(taken, mixer_ref[:, cols], preferred_element_type=f32).astype(jnp.bfloat16).reshape(
            experts, ROWS, WIDE)

    swap_out[...] = picks(1 - c)
    pl.semaphore_wait(barrier, 5 + 2 * (experts - 1))
    swap = remote(swap_out, swap_in, swap_sem.at[0], swap_sem.at[1], sibling)
    swap.start()
    picked[...] = picks(c)
    swap.wait_recv()
    picked[...] = picked[...] + swap_in[...]

    piece = 2 * (z % 2) + c
    to_me = (1 - holder) * (chip) + holder * ((chip % SIDE) * SIDE + chip // SIDE)

    def hop(k):
        e = (z + k) % experts
        return remote(picked.at[e], x.at[holder, to_me, piece], hop_send.at[k], hop_recv.at[piece],
                      {"seq": chip * 2 + holder, "exp": e})

    for k in range(1, experts):
        hop(k).start()

    @pl.when(holder == c)
    def _():
        x[c, me, piece] = picked[z]

    @pl.when(holder != c)
    def _():
        hop(0).start()

    logit_copies = []
    for k in range(1, experts):
        copy = remote(logits_ref, logits_got.at[k - 1], logit_sem.at[0, k], logit_sem.at[1, k],
                      {"exp": (z + k) % experts})
        copy.start()
        logit_copies.append(copy)
    for k in range(4):
        @pl.when((2 * c + k // 2 - z) * (2 * c + k // 2 - z) + (k % 2 - c) * (k % 2 - c) > 0)
        def _(k=k):
            part = x.at[c, me, k]
            remote(part, part, hop_send.at[0], hop_recv.at[k], sibling).wait_recv()

    sent = []

    def spot(d1, d2):
        return ((p2 + 4 - d2) % SIDE) * SIDE + (p1 + 4 - d1) % SIDE

    def whole(d1, d2, n1, n2, device, slot):
        i = spot(d1, d2)
        copy = remote(x.at[c, i], x.at[c, i], ag_send.at[slot], ag_recv.at[n2 * 4 + n1, 0], device)
        copy.start()
        sent.append((ag_send, slot, 4))

    def pair(d1, d2, n1, n2, device, slot, k):
        i = spot(d1, d2)
        part = x.at[c, i, pl.ds(2 * k, 2)]
        copy = remote(part, part, ag_send.at[slot], ag_recv.at[n2 * 4 + n1, k], device)
        copy.start()
        sent.append((ag_send, slot, 2))

    def arrive(d1, d2):
        i = spot(d1, d2)
        if d2 == 2 or (d2 == 0 and d1 == 2):
            for k in range(2):
                part = x.at[c, i, pl.ds(2 * k, 2)]
                remote(part, part, ag_send.at[0], ag_recv.at[d2 * 4 + d1, k], sibling).wait_recv()
        else:
            remote(x.at[c, i], x.at[c, i], ag_send.at[0], ag_recv.at[d2 * 4 + d1, 0], sibling).wait_recv()

    def event(d1, d2):
        if (d1, d2) != (0, 0):
            arrive(d1, d2)
        if d2 == 0:
            if d1 == 0:
                whole(0, 0, 1, 0, right1, 16)
                whole(0, 0, 3, 0, left1, 17)
            elif d1 == 1:
                pair(1, 0, 2, 0, right1, 18, 0)
            elif d1 == 3:
                pair(3, 0, 2, 0, left1, 19, 1)
            whole(d1, 0, d1, 1, right2, d1)
            whole(d1, 0, d1, 3, left2, 4 + d1)
        elif d2 == 1:
            pair(d1, 1, d1, 2, right2, 8 + d1, 0)
        elif d2 == 3:
            pair(d1, 3, d1, 2, left2, 12 + d1, 1)
        i = spot(d1, d2)
        copy = remote(x.at[c, i], x.at[c, i], core_send.at[d2 * 4 + d1], core_recv.at[d2 * 4 + d1], sibling)
        copy.start()
        sent.append((core_send, d2 * 4 + d1, 4))

    def from_sibling(d2):
        for d1 in range(4):
            i = ((p1 + 4 - d2) % SIDE) * SIDE + (p2 + 4 - d1) % SIDE
            part = x.at[1 - c, i]
            remote(part, part, core_send.at[0], core_recv.at[d2 * 4 + d1], sibling).wait_recv()

    events = {
        0: [(0, 0), (1, 0), (3, 0), (0, 1), (0, 3), (2, 0)],
        1: [(1, 1), (1, 3)],
        2: [(3, 1), (3, 3)],
        3: [(2, 1), (2, 3)],
        6: [(0, 2)],
        8: [(1, 2)],
        10: [(3, 2)],
        12: [(2, 2)],
    }
    sibling_groups = {2: 0, 6: 1, 10: 3, 14: 2}

    @pl.loop(0, 16)
    def _(u):
        for when in range(16):
            if when in events or when in sibling_groups or when in (0, 2):
                @pl.when(u == when)
                def _(when=when):
                    for d1, d2 in events.get(when, ()):
                        event(d1, d2)
                    if when in (0, 2):
                        for k in range(4):
                            for n in range(2):
                                weights_in(4 * ((c + when // 2) % 2) + k, n).wait()
                    if when in sibling_groups:
                        from_sibling(sibling_groups[when])
        turn = u // 4
        d2 = turn + turn // 2 - 2 * (turn // 3)
        which = (u // 2) % 2
        half = (c + which) % 2
        base = (((1 - which) * p2 + which * p1 + 4 - d2) % SIDE) * SIDE

        @pl.loop(0, 2)
        def _(kk):
            k = (u % 2) * 2 + kk
            rows = x[half, pl.ds(base, SIDE), k].reshape(SIDE * ROWS, WIDE)
            part = jnp.dot(rows, w_in[half * 4 + k], preferred_element_type=f32)
            part = part.reshape(SIDE, ROWS, 2 * f)

            @pl.when(k == 0)
            def _():
                acc[which, pl.ds(base, SIDE)] = part

            @pl.when(k > 0)
            def _():
                acc[which, pl.ds(base, SIDE)] += part

    @pl.loop(0, 16)
    def _(i):
        flip = (i % SIDE) * SIDE + i // SIDE
        total = acc[0, i] + acc[1, flip]
        gated = total[:, :f]
        value = (gated / (1.0 + jnp.exp(-gated)) * total[:, f:]).astype(jnp.bfloat16)
        hid[0, i] = value
        hid[1, flip] = value

    for sems, slot, size in sent:
        part = x.at[c, 0, pl.ds(0, size)]
        remote(part, part, sems.at[slot], ag_recv.at[0, 0], sibling).wait_send()
    for o in range(8):
        weights_out(o).wait()

    def block(own, d, s):
        return (own + 3 - s) % SIDE if d == 0 else (own + 1 + s) % SIDE

    def q_copy(s, d, jj):
        i = block(p1, d, s) * SIDE + block(p2, d, jj)
        return remote(x.at[1 - c, i, pl.ds(2 * d, 2)], q.at[s, d, jj], q_send.at[s * 8 + d * 4 + jj],
                      q_recv.at[s * 8 + d * 4 + jj], sibling)

    def r1_copy(s, d, jj):
        i = block(p2, d, s) * SIDE + block(p1, d, jj)
        return remote(x.at[c, i, pl.ds(2 * d, 2)], r1.at[s, d, jj], r1_send.at[s * 8 + d * 4 + jj],
                      r1_recv.at[s * 8 + d * 4 + jj], left2 if d else right2)

    def r2_copy(d, jj):
        i = p2 * SIDE + block(p1, d, jj)
        return remote(x.at[c, i, pl.ds(2 * d, 2)], r2.at[jj, d], r2_send.at[jj * 2 + d],
                      r2_recv.at[jj * 2 + d], left1 if d else right1)

    def back_copy(d, core):
        return remote(done.at[2 * d + core], back.at[z, core], back_send.at[2 * d + core], back_recv.at[z],
                      {"seq": chip * 2 + core, "exp": 2 * c + d})

    def is_me(d, core):
        return (2 * c + d - z) * (2 * c + d - z) + (core - c) * (core - c) == 0

    def give_back(d):
        for core in range(2):
            @pl.when(is_me(d, core))
            def _():
                back[z, core] = done[2 * d + core]

            @pl.when(jnp.logical_not(is_me(d, core)))
            def _():
                back_copy(d, core).start()

    def pass_copy(e, core):
        part = back.at[e, core]
        return remote(part, part, pass_send.at[e], pass_recv.at[e], sibling)

    for s in range(4):
        for which in (1, 0):
            half = (c + which) % 2
            own2 = p1 if which else p2
            for d in range(2):
                base = block(own2, d, s) * SIDE

                @pl.loop(0, 2)
                def _(kk):
                    k = 2 * d + kk
                    rows = hid[which, pl.ds(base, SIDE)].reshape(SIDE * ROWS, f)
                    part = jnp.dot(rows, w_out[half * 4 + k], preferred_element_type=f32)
                    x[half, pl.ds(base, SIDE), k] = part.astype(jnp.bfloat16).reshape(SIDE, ROWS, WIDE)

                if which:
                    @pl.loop(0, 4)
                    def _(jj):
                        q_copy(s, d, jj).start()

        def turn(jj):
            for d in range(2):
                i = block(p2, d, s) * SIDE + block(p1, d, jj)
                q_copy(s, d, jj).wait_recv()
                if s > 0:
                    r1_copy(s - 1, d, jj).wait_recv()
                if s == 3 and jj > 0:
                    r2_copy(d, jj - 1).wait_recv()
                for kk in range(2):
                    k = 2 * d + kk
                    total = x[c, i, k].astype(f32) + q[s, d, jj, kk].astype(f32)
                    if s > 0:
                        total = total + r1[s - 1, d, jj, kk].astype(f32)
                    if s == 3 and jj > 0:
                        total = total + r2[jj - 1, d, kk].astype(f32)
                    if s == 3 and jj == 3:
                        done[k] = total.astype(jnp.bfloat16)
                    else:
                        x[c, i, k] = total.astype(jnp.bfloat16)
                if s < 3:
                    r1_copy(s, d, jj).start()
                elif jj < 3:
                    r2_copy(d, jj).start()
                else:
                    give_back(d)

        if s < 3:
            pl.loop(0, 4)(turn)
        else:
            for jj in range(4):
                turn(jj)

    for copy in logit_copies:
        copy.wait_recv()
    logits = logits_ref[...] + logits_got[0] + logits_got[1] + logits_got[2]
    listed = lax.broadcasted_iota(jnp.int32, logits.shape, 0)
    chosen = [
        jnp.sum(jnp.where(jnp.broadcast_to(ids_ref[k : k + 1, :], logits.shape) == listed, logits, 0.0), axis=0,
                keepdims=True)
        for k in range(2)
    ]
    shares = [1.0 / (1.0 + jnp.exp(chosen[1 - k] - chosen[k])) for k in range(2)]
    weight = jnp.where(fits & named0, jnp.broadcast_to(shares[0], spots), 0.0) + jnp.where(
        fits & named1, jnp.broadcast_to(shares[1], spots), 0.0)
    weight = weight.T
    weight_high = weight.astype(jnp.bfloat16)
    weight_low = (weight - weight_high.astype(f32)).astype(jnp.bfloat16)

    for k in range(experts):
        e = (z + k) % experts
        if k == 0:
            @pl.when(holder != c)
            def _():
                part = back.at[z, c]
                remote(part, part, back_send.at[0], back_recv.at[z], sibling).wait_recv()
        else:
            part = back.at[e, c]
            remote(part, part, back_send.at[0], back_recv.at[e], sibling).wait_recv()
        pass_copy(e, c).start()

    def combine(side):
        cols = pl.ds(pl.multiple_of(side * WIDE, WIDE), WIDE)
        rows = jnp.concatenate([back[e, side] for e in range(experts)], axis=0)
        out_ref[:, cols] = (
            mixer_ref[:, cols].astype(f32)
            + jnp.dot(weight_high, rows, preferred_element_type=f32)
            + jnp.dot(weight_low, rows, preferred_element_type=f32)
        )

    combine(c)
    for e in range(experts):
        pass_copy(e, 1 - c).wait_recv()
    combine(1 - c)

    swap.wait_send()
    for k in range(1, experts):
        hop(k).wait_send()

    @pl.when(holder != c)
    def _():
        hop(0).wait_send()

    for copy in logit_copies:
        copy.wait_send()
    for e in range(experts):
        pass_copy(e, c).wait_send()
    for d in range(2):
        for core in range(2):
            @pl.when(jnp.logical_not(is_me(d, core)))
            def _(d=d, core=core):
                back_copy(d, core).wait_send()
    for s in range(4):
        @pl.loop(0, 4)
        def _(jj):
            for d in range(2):
                q_copy(s, d, jj).wait_send()
                if s < 3:
                    r1_copy(s, d, jj).wait_send()
    for jj in range(3):
        for d in range(2):
            r2_copy(d, jj).wait_send()


def experts_layer(mixer_out, logits, ids, w_gate, w_up, w_down):
    f = w_gate.shape[2]
    experts = lax.axis_size("exp")
    bf16, f32 = jnp.bfloat16, jnp.float32
    dma = pltpu.SemaphoreType.DMA
    any_spec = pl.BlockSpec(memory_space=pl.ANY)
    vmem_spec = pl.BlockSpec(memory_space=pltpu.VMEM)
    return pl.pallas_call(
        expert_kernel,
        out_shape=jax.ShapeDtypeStruct(mixer_out.shape, f32),
        in_specs=[vmem_spec, vmem_spec, vmem_spec, any_spec, any_spec, any_spec],
        out_specs=vmem_spec,
        scratch_shapes=[
            pltpu.VMEM((2, 16, 4, ROWS, WIDE), bf16),
            pltpu.VMEM((8, WIDE, 2 * f), bf16),
            pltpu.VMEM((8, f, WIDE), bf16),
            pltpu.VMEM((2, 16, ROWS, 2 * f), f32),
            pltpu.VMEM((2, 16, ROWS, f), bf16),
            pltpu.VMEM((experts, ROWS, WIDE), bf16),
            pltpu.VMEM((experts, ROWS, WIDE), bf16),
            pltpu.VMEM((experts, ROWS, WIDE), bf16),
            pltpu.VMEM((experts - 1,) + logits.shape, f32),
            pltpu.VMEM((4, 2, 4, 2, ROWS, WIDE), bf16),
            pltpu.VMEM((3, 2, 4, 2, ROWS, WIDE), bf16),
            pltpu.VMEM((3, 2, 2, ROWS, WIDE), bf16),
            pltpu.VMEM((4, ROWS, WIDE), bf16),
            pltpu.VMEM((experts, 2, ROWS, WIDE), bf16),
            dma((3, 8)), dma((2,)), dma((4,)), dma((4,)), dma((2, 4)), dma((4,)), dma((4,)), dma((4,)), dma((4,)), dma((20,)), dma((16, 2)), dma((16,)), dma((16,)),
            dma((32,)), dma((32,)), dma((24,)), dma((24,)), dma((6,)), dma((6,)),
        ],
        compiler_params=pltpu.CompilerParams(
            collective_id=0, has_side_effects=True, vmem_limit_bytes=VMEM_LIMIT),
        cost_estimate=pl.CostEstimate(flops=2 * 768 * 8192 * 384 * 3, bytes_accessed=20_000_000, transcendentals=300_000),
    )(mixer_out, logits, ids, w_gate, w_up, w_down)


def on_device(
    inner,
    gate_in,
    w_low,
    w_state,
    w_dt,
    dt_bias,
    decay_rate,
    skip_gain,
    w_router,
    expert_ids,
    w_gate,
    w_up,
    w_down,
):
    mixer_out, logits = mixer(
        inner, gate_in, w_low, w_state, w_dt, dt_bias, decay_rate, skip_gain, w_router
    )
    return experts_layer(mixer_out, logits, expert_ids.T, w_gate, w_up, w_down)


def solution(mesh):
    in_specs = (
        P("seq", "exp"),
        P("seq", "exp"),
        P("exp", None),
        P("exp", None),
        P(None, "exp"),
        P("exp"),
        P("exp", None),
        P("exp"),
        P("exp", None),
        P("seq", None),
        P("exp", None, "seq"),
        P("exp", None, "seq"),
        P("exp", "seq", None),
    )
    out_specs = P("seq", "exp")
    return jax.shard_map(
        on_device, mesh=mesh, in_specs=in_specs, out_specs=out_specs, check_vma=False
    )
```

```python
import functools

import jax
import jax.numpy as jnp
from jax import lax
from jax.experimental import pallas as pl
from jax.experimental.pallas import tpu as pltpu
from jax.sharding import PartitionSpec as P

N = 16
NE = 16
CAP = 24
LANES = 128
LOG2E = 1.4426950408889634
VMEM_LIMIT = 60 * 1024 * 1024


def softplus(v):
    return jnp.maximum(v, 0.0) + jnp.log1p(jnp.exp(-jnp.abs(v)))


def rows_dot(a, b):
    return lax.dot_general(a, b, (((1,), (1,)), ((), ())), preferred_element_type=jnp.float32)


def spread(ref, cols):
    tokens = cols.shape[0]
    for n in range(N):
        ref[pl.ds(n, tokens, stride=N), :] = jnp.broadcast_to(
            cols[:, n : n + 1], (tokens, LANES)
        )

def mixer_kernel(inner_ref, wlow_ref, wstate_ref, bias_ref, decay_ref, skip_ref, wr_ref, wdt_hbm, gate_hbm,
                 mixer_ref, logits_ref,
                 wdt, gate_s, low_part, state_part, low_send, low_got, state_got, low_all, state_all,
                 dt_s, u_s, y_s, b_s, c_s, rate_s, ends, heard, carries, h0,
                 load_sem, low_sem, state_sem, low_sem2, state_sem2, end_sem, carry_sem):
    tokens, channels = inner_ref.shape
    tiles = channels // LANES
    count, experts = lax.axis_size("seq"), lax.axis_size("exp")
    seq, z = lax.axis_index("seq"), lax.axis_index("exp")
    chunk = tokens // experts
    f32, bf16 = jnp.float32, jnp.bfloat16
    mesh_ids = pl.DeviceIdType.MESH

    load_dt = pltpu.make_async_copy(wdt_hbm, wdt, load_sem.at[0])
    load_gate = pltpu.make_async_copy(gate_hbm, gate_s, load_sem.at[1])
    load_dt.start()
    load_gate.start()

    barrier = pltpu.get_barrier_semaphore()
    for k in range(1, experts):
        pl.semaphore_signal(barrier, inc=1, device_id={"exp": (z + k) % experts}, device_id_type=mesh_ids)

    @pl.loop(1, count)
    def _(k):
        pl.semaphore_signal(barrier, inc=1, device_id={"seq": (seq + k) % count}, device_id_type=mesh_ids)

    def remote(src, dst, send, recv, device):
        return pltpu.make_async_remote_copy(
            src_ref=src, dst_ref=dst, send_sem=send, recv_sem=recv, device_id=device, device_id_type=mesh_ids)

    values = inner_ref[...]
    low = jnp.dot(values, wlow_ref[...], preferred_element_type=f32)
    low_part[...] = low.reshape(low_part.shape)
    low_send[...] = low.astype(bf16).reshape(low_send.shape)
    state = rows_dot(values, wstate_ref[...])
    state_part[:, :, : 2 * N] = state.reshape(experts, chunk, 2 * N)
    state_part[:, :, 2 * N :] = jnp.zeros((experts, chunk, LANES - 2 * N), f32)
    for j in range(tiles):
        rate_s[pl.ds(j, N, stride=tiles), :] = decay_ref[:, pl.ds(j * LANES, LANES)] * -LOG2E
    pl.semaphore_wait(barrier, experts - 1 + count - 1)
    first = []
    for k in range(1, experts):
        to = (z + k) % experts
        first.append(remote(low_send.at[to], low_got.at[k - 1], low_sem.at[0, k], low_sem.at[1, k], {"exp": to}))
        first.append(remote(state_part.at[to], state_got.at[k - 1], state_sem.at[0, k], state_sem.at[1, k], {"exp": to}))
    for copy in first:
        copy.start()
    for copy in first:
        copy.wait_recv()
    low_sum, state_sum = low_part[z], state_part[z]
    for k in range(1, experts):
        low_sum = low_sum + low_got[k - 1].astype(f32)
        state_sum = state_sum + state_got[k - 1]
    low_all[z] = low_sum.astype(bf16)
    state_all[z] = state_sum
    second = []
    for k in range(1, experts):
        to = {"exp": (z + k) % experts}
        second.append(remote(low_all.at[z], low_all.at[z], low_sem2.at[0, k], low_sem2.at[1, k], to))
        second.append(remote(state_all.at[z], state_all.at[z], state_sem2.at[0, k], state_sem2.at[1, k], to))
    for copy in second:
        copy.start()
    for copy in second:
        copy.wait_recv()

    load_dt.wait()
    low_b = low_all[...].reshape(tokens, low_all.shape[2])
    for j in range(channels // 256):
        cols = pl.ds(j * 256, 256)
        dt = softplus(jnp.dot(low_b, wdt[:, cols], preferred_element_type=f32) + bias_ref[:, cols])
        u = dt * inner_ref[:, cols].astype(f32)
        for k in range(2):
            part = slice(k * LANES, (k + 1) * LANES)
            dt_s[pl.ds(2 * j + k, tokens, stride=tiles), :] = dt[:, part]
            u_s[pl.ds(2 * j + k, tokens, stride=tiles), :] = u[:, part]
    maps = state_all[...].reshape(tokens, LANES)
    spread(b_s, maps[:, :N])
    for half in range(2):
        rate = [rate_s[pl.ds(n * tiles + half * 8, 8), :] for n in range(N)]

        def step(t, carry):
            total, h = carry
            at = pl.multiple_of(t * tiles + half * 8, 8)
            dt = dt_s[pl.ds(at, 8), :]
            u = u_s[pl.ds(at, 8), :]
            new = []
            for n in range(N):
                b = b_s[pl.ds(t * N + n, 1), :]
                new.append(jnp.exp2(dt * rate[n]) * h[n] + u * b)
            return total + dt, tuple(new)

        zero = jnp.zeros((8, LANES), f32)
        total, h = lax.fori_loop(0, tokens, step, (zero, (zero,) * N), unroll=4)
        for n in range(N):
            ends[2 * n + half, 0] = jnp.exp2(total * rate[n])
            ends[2 * n + half, 1] = h[n]

    @pl.loop(1, count)
    def _(k):
        to = (seq + k) % count
        remote(ends.at[to], heard.at[seq], end_sem.at[0], end_sem.at[1], {"seq": to}).start()

    heard[seq] = ends[seq]
    spread(c_s, maps[:, N : 2 * N])
    others = pl.ds(0, count - 1)
    remote(ends.at[others], heard.at[others], end_sem.at[0], end_sem.at[1], {"seq": (seq + 1) % count}).wait()

    def join(s, carry):
        carries[s] = carry
        return heard[s, 0] * carry + heard[s, 1]

    lax.fori_loop(0, count, join, jnp.zeros((8, LANES), f32), unroll=4)

    @pl.loop(1, count)
    def _(k):
        to = (seq + k) % count
        remote(carries.at[to], h0.at[seq], carry_sem.at[0], carry_sem.at[1], {"seq": to}).start()

    h0[seq] = carries[seq]
    remote(carries.at[others], h0.at[others], carry_sem.at[0], carry_sem.at[1], {"seq": (seq + 1) % count}).wait()

    for half in range(2):
        rate = [rate_s[pl.ds(n * tiles + half * 8, 8), :] for n in range(N)]

        def step(t, h):
            at = pl.multiple_of(t * tiles + half * 8, 8)
            dt = dt_s[pl.ds(at, 8), :]
            u = u_s[pl.ds(at, 8), :]
            new = []
            y = None
            for n in range(N):
                b = b_s[pl.ds(t * N + n, 1), :]
                c = c_s[pl.ds(t * N + n, 1), :]
                new.append(jnp.exp2(dt * rate[n]) * h[n] + u * b)
                y = new[n] * c if y is None else y + new[n] * c
            y_s[pl.ds(at, 8), :] = y
            return tuple(new)

        lax.fori_loop(0, tokens, step, tuple(h0[2 * n + half] for n in range(N)), unroll=4)
    load_gate.wait()
    for j in range(tiles):
        cols = pl.ds(j * LANES, LANES)
        y = y_s[pl.ds(j, tokens, stride=tiles), :]
        gate = gate_s[:, cols].astype(f32)
        value = (y + skip_ref[:, cols] * inner_ref[:, cols].astype(f32)) * (gate / (1.0 + jnp.exp(-gate)))
        mixer_ref[:, cols] = value.astype(bf16)
    logits_ref[...] = rows_dot(wr_ref[...], mixer_ref[...])
    for copy in first + second:
        copy.wait_send()


def mixer(inner, gate_in, w_low, w_state, w_dt, dt_bias, decay_rate, skip_gain, w_router):
    tokens, channels = inner.shape
    rank = w_low.shape[1]
    tiles = channels // LANES
    count, experts = lax.axis_size("seq"), lax.axis_size("exp")
    chunk = tokens // experts
    f32, bf16 = jnp.float32, jnp.bfloat16
    dma = pltpu.SemaphoreType.DMA
    any_spec = pl.BlockSpec(memory_space=pl.ANY)
    vmem_spec = pl.BlockSpec(memory_space=pltpu.VMEM)
    return pl.pallas_call(
        mixer_kernel,
        out_shape=(
            jax.ShapeDtypeStruct((tokens, channels), bf16),
            jax.ShapeDtypeStruct((NE, tokens), f32),
        ),
        in_specs=[vmem_spec] * 7 + [any_spec] * 2,
        out_specs=(vmem_spec, vmem_spec),
        scratch_shapes=[
            pltpu.VMEM(w_dt.shape, bf16),
            pltpu.VMEM((tokens, channels), bf16),
            pltpu.VMEM((experts, chunk, rank), f32),
            pltpu.VMEM((experts, chunk, LANES), f32),
            pltpu.VMEM((experts, chunk, rank), bf16),
            pltpu.VMEM((experts - 1, chunk, rank), bf16),
            pltpu.VMEM((experts - 1, chunk, LANES), f32),
            pltpu.VMEM((experts, chunk, rank), bf16),
            pltpu.VMEM((experts, chunk, LANES), f32),
        ]
        + [pltpu.VMEM((tokens * tiles, LANES), f32)] * 3
        + [pltpu.VMEM((tokens * N, LANES), f32)] * 2
        + [pltpu.VMEM((N * tiles, LANES), f32)]
        + [pltpu.VMEM((count, 2, 8, LANES), f32)] * 2
        + [pltpu.VMEM((count, 8, LANES), f32)] * 2
        + [dma((2,))] + [dma((2, experts))] * 4 + [dma((2,))] * 2,
        compiler_params=pltpu.CompilerParams(
            collective_id=1, has_side_effects=True, vmem_limit_bytes=VMEM_LIMIT),
    )(inner, w_low, w_state.T, dt_bias[None], decay_rate.T, skip_gain[None], w_router.T, w_dt, gate_in)


ROWS = 2 * CAP
WIDE = 1024
SIDE = 4


def expert_kernel(mixer_ref, logits_ref, ids_ref, gate_ref, up_ref, down_ref, out_ref,
                  x, w_in, w_out, acc, hid, hid_out, swap_out, swap_in, picked, logits_got, r1, r2, done, back,
                  w_sem, swap_sem, hop_send, hop_recv, logit_sem, back_send, back_recv, pass_send, pass_recv, ag_send, ag_recv, core_send, core_recv,
                  push_send, push_recv, hid_sem, r1_send, r1_recv, r2_send, r2_recv):
    seq, z = lax.axis_index("seq"), lax.axis_index("exp")
    experts = lax.axis_size("exp")
    tokens = mixer_ref.shape[0]
    c = seq % 2
    chip = seq // 2
    holder = z // 2
    f = gate_ref.shape[2]
    f32 = jnp.float32
    p1 = (1 - c) * (chip % SIDE) + c * (chip // SIDE)
    p2 = (1 - c) * (chip // SIDE) + c * (chip % SIDE)
    me = p2 * SIDE + p1

    def at(i1, i2, core=None):
        where = (1 - c) * (i2 * SIDE + i1) + c * (i1 * SIDE + i2)
        return {"seq": where * 2 + (c if core is None else core)}

    sibling = at(p1, p2, 1 - c)
    right1, left1 = at((p1 + 1) % SIDE, p2), at((p1 + 3) % SIDE, p2)
    right2, left2 = at(p1, (p2 + 1) % SIDE), at(p1, (p2 + 3) % SIDE)

    def remote(src, dst, send, recv, device):
        return pltpu.make_async_remote_copy(
            src_ref=src, dst_ref=dst, send_sem=send, recv_sem=recv,
            device_id=device, device_id_type=pl.DeviceIdType.MESH)

    def weights_in(o, n):
        return pltpu.make_async_copy(
            (gate_ref, up_ref)[n].at[0, pl.ds(o * WIDE, WIDE), :], w_in.at[o // 2, pl.ds((o % 2) * WIDE, WIDE), pl.ds(n * f, f)], w_sem.at[n, o])

    def weights_out(k):
        return pltpu.make_async_copy(
            down_ref.at[0, :, pl.ds((4 * c + k) * WIDE, WIDE)], w_out.at[k, pl.ds(0, f)], w_sem.at[2, k])

    def push(k):
        return remote(down_ref.at[0, :, pl.ds((4 * (1 - c) + k) * WIDE, WIDE)], w_out.at[k, pl.ds(f, f)],
                      push_send.at[k], push_recv.at[k], sibling)

    for o in range(8):
        for n in range(2):
            weights_in((4 * c + o) % 8, n).start()
    for k in range(4):
        weights_out(k).start()

    barrier = pltpu.get_barrier_semaphore()
    for peer in (sibling, right1, left1, right2, left2, at((p1 + 2) % SIDE, p2)):
        pl.semaphore_signal(barrier, inc=1, device_id=peer, device_id_type=pl.DeviceIdType.MESH)
    for core in range(2):
        for k in range(1, experts):
            peer = {"seq": chip * 2 + core, "exp": (z + k) % experts}
            pl.semaphore_signal(barrier, inc=1, device_id=peer, device_id_type=pl.DeviceIdType.MESH)

    spots = (experts * ROWS, tokens)
    row = lax.broadcasted_iota(jnp.int32, spots, 0)
    one, none = jnp.ones(spots, jnp.int32), jnp.zeros(spots, jnp.int32)
    expert = none
    for e in range(1, experts):
        expert = expert + jnp.where(row >= e * ROWS, one, none)
    row = row - ROWS * expert
    core_of = jnp.where(row >= CAP, one, none)
    slot = row - CAP * core_of
    named0 = jnp.broadcast_to(ids_ref[0:1, :], spots) == expert
    named1 = jnp.broadcast_to(ids_ref[1:2, :], spots) == expert
    load = jnp.where(named0 | named1, 1.0, 0.0)
    before = jnp.where(
        lax.broadcasted_iota(jnp.int32, (tokens, tokens), 0) < lax.broadcasted_iota(jnp.int32, (tokens, tokens), 1),
        1.0, 0.0).astype(jnp.bfloat16)
    earlier = jnp.dot(load.astype(jnp.bfloat16), before, preferred_element_type=f32)
    fits = (earlier == slot.astype(f32)) & (core_of == c)
    taken = jnp.where(fits, load, 0.0).astype(jnp.bfloat16)

    def picks(side):
        cols = pl.ds(pl.multiple_of(side * WIDE, WIDE), WIDE)
        return jnp.dot(taken, mixer_ref[:, cols], preferred_element_type=f32).astype(jnp.bfloat16).reshape(
            experts, ROWS, WIDE)

    swap_out[...] = picks(1 - c)
    pl.semaphore_wait(barrier, 6 + 2 * (experts - 1))
    swap = remote(swap_out, swap_in, swap_sem.at[0], swap_sem.at[1], sibling)
    swap.start()
    picked[...] = picks(c)
    swap.wait_recv()
    picked[...] = picked[...] + swap_in[...]

    piece = 2 * (z % 2) + c
    to_me = (1 - holder) * (chip) + holder * ((chip % SIDE) * SIDE + chip // SIDE)

    def hop(k):
        e = (z + k) % experts
        return remote(picked.at[e], x.at[holder, to_me, piece], hop_send.at[k], hop_recv.at[piece],
                      {"seq": chip * 2 + holder, "exp": e})

    for k in range(1, experts):
        hop(k).start()

    @pl.when(holder == c)
    def _():
        x[c, me, piece] = picked[z]

    @pl.when(holder != c)
    def _():
        hop(0).start()

    for k in range(4):
        push(k).start()
    logit_copies = []
    for k in range(1, experts):
        copy = remote(logits_ref, logits_got.at[k - 1], logit_sem.at[0, k], logit_sem.at[1, k],
                      {"exp": (z + k) % experts})
        copy.start()
        logit_copies.append(copy)
    for k in range(4):
        @pl.when((2 * c + k // 2 - z) * (2 * c + k // 2 - z) + (k % 2 - c) * (k % 2 - c) > 0)
        def _(k=k):
            part = x.at[c, me, k]
            remote(part, part, hop_send.at[0], hop_recv.at[k], sibling).wait_recv()

    sent = []

    def spot(d1, d2):
        return ((p2 + 4 - d2) % SIDE) * SIDE + (p1 + 4 - d1) % SIDE

    def whole(d1, d2, n1, n2, device, slot):
        i = spot(d1, d2)
        copy = remote(x.at[c, i], x.at[c, i], ag_send.at[slot], ag_recv.at[n2 * 4 + n1, 0], device)
        copy.start()
        sent.append((ag_send, slot, 4))

    def pair(d1, d2, n1, n2, device, slot, k):
        i = spot(d1, d2)
        part = x.at[c, i, pl.ds(2 * k, 2)]
        copy = remote(part, part, ag_send.at[slot], ag_recv.at[n2 * 4 + n1, k], device)
        copy.start()
        sent.append((ag_send, slot, 2))

    def arrive(d1, d2):
        i = spot(d1, d2)
        if d2 == 2 or (d2 == 0 and d1 == 2):
            for k in range(2):
                part = x.at[c, i, pl.ds(2 * k, 2)]
                remote(part, part, ag_send.at[0], ag_recv.at[d2 * 4 + d1, k], sibling).wait_recv()
        else:
            remote(x.at[c, i], x.at[c, i], ag_send.at[0], ag_recv.at[d2 * 4 + d1, 0], sibling).wait_recv()

    def event(d1, d2):
        if (d1, d2) != (0, 0):
            arrive(d1, d2)
        if d2 == 0:
            if d1 == 0:
                whole(0, 0, 1, 0, right1, 16)
                whole(0, 0, 3, 0, left1, 17)
            elif d1 == 1:
                pair(1, 0, 2, 0, right1, 18, 0)
            elif d1 == 3:
                pair(3, 0, 2, 0, left1, 19, 1)
            whole(d1, 0, d1, 1, right2, d1)
            whole(d1, 0, d1, 3, left2, 4 + d1)
        elif d2 == 1:
            pair(d1, 1, d1, 2, right2, 8 + d1, 0)
        elif d2 == 3:
            pair(d1, 3, d1, 2, left2, 12 + d1, 1)
        i = spot(d1, d2)
        copy = remote(x.at[c, i], x.at[c, i], core_send.at[d2 * 4 + d1], core_recv.at[d2 * 4 + d1], sibling)
        copy.start()
        sent.append((core_send, d2 * 4 + d1, 4))

    def from_sibling(d2):
        for d1 in range(4):
            i = ((p1 + 4 - d2) % SIDE) * SIDE + (p2 + 4 - d1) % SIDE
            part = x.at[1 - c, i]
            remote(part, part, core_send.at[0], core_recv.at[d2 * 4 + d1], sibling).wait_recv()

    events = {
        0: [(0, 0), (1, 0), (3, 0), (0, 1), (0, 3), (2, 0)],
        1: [(1, 1), (1, 3)],
        2: [(3, 1), (3, 3)],
        3: [(2, 1), (2, 3)],
        6: [(0, 2)],
        8: [(1, 2)],
        10: [(3, 2)],
        12: [(2, 2)],
    }
    sibling_groups = {2: 0, 6: 1, 10: 3, 14: 2}

    @pl.loop(0, 16)
    def _(u):
        for when in range(16):
            if when in events or when in sibling_groups or when in (0, 2):
                @pl.when(u == when)
                def _(when=when):
                    for d1, d2 in events.get(when, ()):
                        event(d1, d2)
                    if when in (0, 2):
                        for k in range(4):
                            for n in range(2):
                                weights_in(4 * ((c + when // 2) % 2) + k, n).wait()
                    if when in sibling_groups:
                        from_sibling(sibling_groups[when])
        turn = u // 4
        d2 = turn + turn // 2 - 2 * (turn // 3)
        which = (u // 2) % 2
        half = (c + which) % 2
        base = (((1 - which) * p2 + which * p1 + 4 - d2) % SIDE) * SIDE

        side = u % 2
        rows = jnp.concatenate(
            [x[half, pl.ds(base, SIDE), 2 * side + k].reshape(SIDE * ROWS, WIDE) for k in range(2)], axis=1)
        part = jnp.dot(rows, w_in[half * 2 + side], preferred_element_type=f32).reshape(SIDE, ROWS, 2 * f)

        @pl.when(side == 0)
        def _():
            acc[which, pl.ds(base, SIDE)] = part

        @pl.when(side > 0)
        def _():
            acc[which, pl.ds(base, SIDE)] += part

    @pl.loop(0, 16)
    def _(i):
        flip = (i % SIDE) * SIDE + i // SIDE
        total = acc[0, i] + acc[1, flip]
        gated = total[:, :f]
        value = (gated / (1.0 + jnp.exp(-gated)) * total[:, f:]).astype(jnp.bfloat16)
        hid[0, i] = value
        hid_out[flip] = value
        remote(hid_out.at[flip], hid.at[1, flip], hid_sem.at[0], hid_sem.at[1], sibling).start()

    for sems, slot, size in sent:
        part = x.at[c, 0, pl.ds(0, size)]
        remote(part, part, sems.at[slot], ag_recv.at[0, 0], sibling).wait_send()
    for k in range(4):
        weights_out(k).wait()
        push(k).wait()
    remote(hid_out, hid.at[1], hid_sem.at[0], hid_sem.at[1], sibling).wait()

    def block(own, d, s):
        return (own + 3 - s) % SIDE if d == 0 else (own + 1 + s) % SIDE

    def r1_copy(s, d, jj):
        i = block(p2, d, s) * SIDE + block(p1, d, jj)
        return remote(x.at[c, i, pl.ds(2 * d, 2)], r1.at[s, d, jj], r1_send.at[s * 8 + d * 4 + jj],
                      r1_recv.at[s * 8 + d * 4 + jj], left2 if d else right2)

    def r2_copy(d, jj):
        i = p2 * SIDE + block(p1, d, jj)
        return remote(x.at[c, i, pl.ds(2 * d, 2)], r2.at[jj, d], r2_send.at[jj * 2 + d],
                      r2_recv.at[jj * 2 + d], at(block(p1, d, jj), p2))

    def back_copy(d, core):
        return remote(done.at[2 * d + core], back.at[z, core], back_send.at[2 * d + core], back_recv.at[z],
                      {"seq": chip * 2 + core, "exp": 2 * c + d})

    def is_me(d, core):
        return (2 * c + d - z) * (2 * c + d - z) + (core - c) * (core - c) == 0

    def give_back(d):
        for core in range(2):
            @pl.when(is_me(d, core))
            def _():
                back[z, core] = done[2 * d + core]

            @pl.when(jnp.logical_not(is_me(d, core)))
            def _():
                back_copy(d, core).start()

    def pass_copy(e, core):
        part = back.at[e, core]
        return remote(part, part, pass_send.at[e], pass_recv.at[e], sibling)

    for s in range(4):
        for d in range(2):
            base = block(p2, d, s) * SIDE

            @pl.loop(0, 2)
            def _(kk):
                k = 2 * d + kk
                rows = jnp.concatenate(
                    [hid[n, pl.ds(base, SIDE)].reshape(SIDE * ROWS, f) for n in range(2)], axis=1)
                part = jnp.dot(rows, w_out[k], preferred_element_type=f32)
                x[c, pl.ds(base, SIDE), k] = part.astype(jnp.bfloat16).reshape(SIDE, ROWS, WIDE)

        def turn(jj):
            for d in range(2):
                i = block(p2, d, s) * SIDE + block(p1, d, jj)
                if s > 0:
                    r1_copy(s - 1, d, jj).wait_recv()
                if s == 3 and jj == 3:
                    for other in range(3):
                        r2_copy(d, other).wait_recv()
                for kk in range(2 if s > 0 else 0):
                    k = 2 * d + kk
                    total = x[c, i, k].astype(f32) + r1[s - 1, d, jj, kk].astype(f32)
                    if s == 3 and jj == 3:
                        for other in range(3):
                            total = total + r2[other, d, kk].astype(f32)
                    if s == 3 and jj == 3:
                        done[k] = total.astype(jnp.bfloat16)
                    else:
                        x[c, i, k] = total.astype(jnp.bfloat16)
                if s < 3:
                    r1_copy(s, d, jj).start()
                elif jj < 3:
                    r2_copy(d, jj).start()
                else:
                    give_back(d)

        if s < 3:
            pl.loop(0, 4)(turn)
        else:
            for jj in range(4):
                turn(jj)

    for copy in logit_copies:
        copy.wait_recv()
    logits = logits_ref[...] + logits_got[0] + logits_got[1] + logits_got[2]
    listed = lax.broadcasted_iota(jnp.int32, logits.shape, 0)
    chosen = [
        jnp.sum(jnp.where(jnp.broadcast_to(ids_ref[k : k + 1, :], logits.shape) == listed, logits, 0.0), axis=0,
                keepdims=True)
        for k in range(2)
    ]
    shares = [1.0 / (1.0 + jnp.exp(chosen[1 - k] - chosen[k])) for k in range(2)]
    weight = jnp.where(fits & named0, jnp.broadcast_to(shares[0], spots), 0.0) + jnp.where(
        fits & named1, jnp.broadcast_to(shares[1], spots), 0.0)
    weight = weight.T
    weight_high = weight.astype(jnp.bfloat16)
    weight_low = (weight - weight_high.astype(f32)).astype(jnp.bfloat16)

    for k in range(experts):
        e = (z + k) % experts
        if k == 0:
            @pl.when(holder != c)
            def _():
                part = back.at[z, c]
                remote(part, part, back_send.at[0], back_recv.at[z], sibling).wait_recv()
        else:
            part = back.at[e, c]
            remote(part, part, back_send.at[0], back_recv.at[e], sibling).wait_recv()
        pass_copy(e, c).start()

    def combine(side):
        cols = pl.ds(pl.multiple_of(side * WIDE, WIDE), WIDE)
        rows = jnp.concatenate([back[e, side] for e in range(experts)], axis=0)
        out_ref[:, cols] = (
            mixer_ref[:, cols].astype(f32)
            + jnp.dot(weight_high, rows, preferred_element_type=f32)
            + jnp.dot(weight_low, rows, preferred_element_type=f32)
        )

    combine(c)
    for e in range(experts):
        pass_copy(e, 1 - c).wait_recv()
    combine(1 - c)

    swap.wait_send()
    for k in range(1, experts):
        hop(k).wait_send()

    @pl.when(holder != c)
    def _():
        hop(0).wait_send()

    for copy in logit_copies:
        copy.wait_send()
    for e in range(experts):
        pass_copy(e, c).wait_send()
    for d in range(2):
        for core in range(2):
            @pl.when(jnp.logical_not(is_me(d, core)))
            def _(d=d, core=core):
                back_copy(d, core).wait_send()
    for s in range(3):
        @pl.loop(0, 4)
        def _(jj):
            for d in range(2):
                r1_copy(s, d, jj).wait_send()
    for jj in range(3):
        for d in range(2):
            r2_copy(d, jj).wait_send()


def experts_layer(mixer_out, logits, ids, w_gate, w_up, w_down):
    f = w_gate.shape[2]
    experts = lax.axis_size("exp")
    bf16, f32 = jnp.bfloat16, jnp.float32
    dma = pltpu.SemaphoreType.DMA
    any_spec = pl.BlockSpec(memory_space=pl.ANY)
    vmem_spec = pl.BlockSpec(memory_space=pltpu.VMEM)
    return pl.pallas_call(
        expert_kernel,
        out_shape=jax.ShapeDtypeStruct(mixer_out.shape, f32),
        in_specs=[vmem_spec, vmem_spec, vmem_spec, any_spec, any_spec, any_spec],
        out_specs=vmem_spec,
        scratch_shapes=[
            pltpu.VMEM((2, 16, 4, ROWS, WIDE), bf16),
            pltpu.VMEM((4, 2 * WIDE, 2 * f), bf16),
            pltpu.VMEM((4, 2 * f, WIDE), bf16),
            pltpu.VMEM((2, 16, ROWS, 2 * f), f32),
            pltpu.VMEM((2, 16, ROWS, f), bf16),
            pltpu.VMEM((16, ROWS, f), bf16),
            pltpu.VMEM((experts, ROWS, WIDE), bf16),
            pltpu.VMEM((experts, ROWS, WIDE), bf16),
            pltpu.VMEM((experts, ROWS, WIDE), bf16),
            pltpu.VMEM((experts - 1,) + logits.shape, f32),
            pltpu.VMEM((3, 2, 4, 2, ROWS, WIDE), bf16),
            pltpu.VMEM((3, 2, 2, ROWS, WIDE), bf16),
            pltpu.VMEM((4, ROWS, WIDE), bf16),
            pltpu.VMEM((experts, 2, ROWS, WIDE), bf16),
            dma((3, 8)), dma((2,)), dma((4,)), dma((4,)), dma((2, 4)), dma((4,)), dma((4,)), dma((4,)), dma((4,)), dma((20,)), dma((16, 2)), dma((16,)), dma((16,)),
            dma((4,)), dma((4,)), dma((2,)), dma((24,)), dma((24,)), dma((6,)), dma((6,)),
        ],
        compiler_params=pltpu.CompilerParams(
            collective_id=0, has_side_effects=True, vmem_limit_bytes=VMEM_LIMIT),
        cost_estimate=pl.CostEstimate(flops=2 * 768 * 8192 * 384 * 3, bytes_accessed=20_000_000, transcendentals=300_000),
    )(mixer_out, logits, ids, w_gate, w_up, w_down)


def on_device(
    inner,
    gate_in,
    w_low,
    w_state,
    w_dt,
    dt_bias,
    decay_rate,
    skip_gain,
    w_router,
    expert_ids,
    w_gate,
    w_up,
    w_down,
):
    mixer_out, logits = mixer(
        inner, gate_in, w_low, w_state, w_dt, dt_bias, decay_rate, skip_gain, w_router
    )
    return experts_layer(mixer_out, logits, expert_ids.T, w_gate, w_up, w_down)


def solution(mesh):
    in_specs = (
        P("seq", "exp"),
        P("seq", "exp"),
        P("exp", None),
        P("exp", None),
        P(None, "exp"),
        P("exp"),
        P("exp", None),
        P("exp"),
        P("exp", None),
        P("seq", None),
        P("exp", None, "seq"),
        P("exp", None, "seq"),
        P("exp", "seq", None),
    )
    out_specs = P("seq", "exp")
    return jax.shard_map(
        on_device, mesh=mesh, in_specs=in_specs, out_specs=out_specs, check_vma=False
    )
```

```python
import functools

import jax
import jax.numpy as jnp
from jax import lax
from jax.experimental import pallas as pl
from jax.experimental.pallas import tpu as pltpu
from jax.sharding import PartitionSpec as P

N = 16
NE = 16
CAP = 24
LANES = 128
LOG2E = 1.4426950408889634
VMEM_LIMIT = 60 * 1024 * 1024


def softplus(v):
    return jnp.maximum(v, 0.0) + jnp.log1p(jnp.exp(-jnp.abs(v)))


def rows_dot(a, b):
    return lax.dot_general(a, b, (((1,), (1,)), ((), ())), preferred_element_type=jnp.float32)


def spread(ref, cols):
    tokens = cols.shape[0]
    for n in range(N):
        ref[pl.ds(n, tokens, stride=N), :] = jnp.broadcast_to(
            cols[:, n : n + 1], (tokens, LANES)
        )

def mixer_kernel(inner_ref, wlow_ref, wstate_ref, bias_ref, decay_ref, skip_ref, wr_ref, wdt_hbm, gate_hbm,
                 mixer_ref, logits_ref,
                 wdt, gate_s, silu_s, low_part, state_part, low_send, low_got, state_got, low_all, state_all,
                 dt_s, u_s, y_s, b_s, c_s, rate_s, ends, heard, carries, h0,
                 load_sem, low_sem, state_sem, low_sem2, state_sem2, end_sem, carry_sem):
    tokens, channels = inner_ref.shape
    tiles = channels // LANES
    count, experts = lax.axis_size("seq"), lax.axis_size("exp")
    seq, z = lax.axis_index("seq"), lax.axis_index("exp")
    chunk = tokens // experts
    f32, bf16 = jnp.float32, jnp.bfloat16
    mesh_ids = pl.DeviceIdType.MESH

    load_dt = pltpu.make_async_copy(wdt_hbm, wdt, load_sem.at[0])
    load_gate = pltpu.make_async_copy(gate_hbm, gate_s, load_sem.at[1])
    load_dt.start()
    load_gate.start()

    barrier = pltpu.get_barrier_semaphore()
    for k in range(1, experts):
        pl.semaphore_signal(barrier, inc=1, device_id={"exp": (z + k) % experts}, device_id_type=mesh_ids)

    @pl.loop(1, count)
    def _(k):
        pl.semaphore_signal(barrier, inc=1, device_id={"seq": (seq + k) % count}, device_id_type=mesh_ids)

    def remote(src, dst, send, recv, device):
        return pltpu.make_async_remote_copy(
            src_ref=src, dst_ref=dst, send_sem=send, recv_sem=recv, device_id=device, device_id_type=mesh_ids)

    values = inner_ref[...]
    low = jnp.dot(values, wlow_ref[...], preferred_element_type=f32)
    low_part[...] = low.reshape(low_part.shape)
    low_send[...] = low.astype(bf16).reshape(low_send.shape)
    state = rows_dot(values, wstate_ref[...])
    state_part[:, :, : 2 * N] = state.reshape(experts, chunk, 2 * N)
    state_part[:, :, 2 * N :] = jnp.zeros((experts, chunk, LANES - 2 * N), f32)
    for j in range(tiles):
        rate_s[pl.ds(j, N, stride=tiles), :] = decay_ref[:, pl.ds(j * LANES, LANES)] * -LOG2E
    pl.semaphore_wait(barrier, experts - 1 + count - 1)
    first = []
    for k in range(1, experts):
        to = (z + k) % experts
        first.append(remote(low_send.at[to], low_got.at[k - 1], low_sem.at[0, k], low_sem.at[1, k], {"exp": to}))
        first.append(remote(state_part.at[to], state_got.at[k - 1], state_sem.at[0, k], state_sem.at[1, k], {"exp": to}))
    for copy in first:
        copy.start()
    for copy in first:
        copy.wait_recv()
    low_sum, state_sum = low_part[z], state_part[z]
    for k in range(1, experts):
        low_sum = low_sum + low_got[k - 1].astype(f32)
        state_sum = state_sum + state_got[k - 1]
    low_all[z] = low_sum.astype(bf16)
    state_all[z] = state_sum
    second = []
    for k in range(1, experts):
        to = {"exp": (z + k) % experts}
        second.append(remote(low_all.at[z], low_all.at[z], low_sem2.at[0, k], low_sem2.at[1, k], to))
        second.append(remote(state_all.at[z], state_all.at[z], state_sem2.at[0, k], state_sem2.at[1, k], to))
    for copy in second:
        copy.start()
    for copy in second:
        copy.wait_recv()

    load_dt.wait()
    low_b = low_all[...].reshape(tokens, low_all.shape[2])
    for j in range(channels // 256):
        cols = pl.ds(j * 256, 256)
        dt = softplus(jnp.dot(low_b, wdt[:, cols], preferred_element_type=f32) + bias_ref[:, cols])
        u = dt * inner_ref[:, cols].astype(f32)
        for k in range(2):
            part = slice(k * LANES, (k + 1) * LANES)
            dt_s[pl.ds(2 * j + k, tokens, stride=tiles), :] = dt[:, part]
            u_s[pl.ds(2 * j + k, tokens, stride=tiles), :] = u[:, part]
    maps = state_all[...].reshape(tokens, LANES)
    spread(b_s, maps[:, :N])
    for half in range(2):
        rate = [rate_s[pl.ds(n * tiles + half * 8, 8), :] for n in range(N)]

        def step(t, carry):
            total, h = carry
            at = pl.multiple_of(t * tiles + half * 8, 8)
            dt = dt_s[pl.ds(at, 8), :]
            u = u_s[pl.ds(at, 8), :]
            new = []
            for n in range(N):
                b = b_s[pl.ds(t * N + n, 1), :]
                new.append(jnp.exp2(dt * rate[n]) * h[n] + u * b)
            return total + dt, tuple(new)

        zero = jnp.zeros((8, LANES), f32)
        total, h = lax.fori_loop(0, tokens, step, (zero, (zero,) * N), unroll=4)
        for n in range(N):
            ends[2 * n + half, 0] = jnp.exp2(total * rate[n])
            ends[2 * n + half, 1] = h[n]

    @pl.loop(1, count)
    def _(k):
        to = (seq + k) % count
        remote(ends.at[to], heard.at[seq], end_sem.at[0], end_sem.at[1], {"seq": to}).start()

    heard[seq] = ends[seq]
    spread(c_s, maps[:, N : 2 * N])
    others = pl.ds(0, count - 1)
    remote(ends.at[others], heard.at[others], end_sem.at[0], end_sem.at[1], {"seq": (seq + 1) % count}).wait()

    def join(s, carry):
        carries[s] = carry
        return heard[s, 0] * carry + heard[s, 1]

    lax.fori_loop(0, count, join, jnp.zeros((8, LANES), f32), unroll=4)

    @pl.loop(1, count)
    def _(k):
        to = (seq + k) % count
        remote(carries.at[to], h0.at[seq], carry_sem.at[0], carry_sem.at[1], {"seq": to}).start()

    h0[seq] = carries[seq]
    load_gate.wait()
    for j in range(tiles):
        cols = pl.ds(j * LANES, LANES)
        gate = gate_s[:, cols].astype(f32)
        silu_s[:, cols] = gate / (1.0 + jnp.exp(-gate))
    remote(carries.at[others], h0.at[others], carry_sem.at[0], carry_sem.at[1], {"seq": (seq + 1) % count}).wait()

    for half in range(2):
        rate = [rate_s[pl.ds(n * tiles + half * 8, 8), :] for n in range(N)]

        def step(t, h):
            at = pl.multiple_of(t * tiles + half * 8, 8)
            dt = dt_s[pl.ds(at, 8), :]
            u = u_s[pl.ds(at, 8), :]
            new = []
            y = None
            for n in range(N):
                b = b_s[pl.ds(t * N + n, 1), :]
                c = c_s[pl.ds(t * N + n, 1), :]
                new.append(jnp.exp2(dt * rate[n]) * h[n] + u * b)
                y = new[n] * c if y is None else y + new[n] * c
            y_s[pl.ds(at, 8), :] = y
            return tuple(new)

        lax.fori_loop(0, tokens, step, tuple(h0[2 * n + half] for n in range(N)), unroll=4)
    for j in range(tiles):
        cols = pl.ds(j * LANES, LANES)
        y = y_s[pl.ds(j, tokens, stride=tiles), :]
        value = (y + skip_ref[:, cols] * inner_ref[:, cols].astype(f32)) * silu_s[:, cols]
        mixer_ref[:, cols] = value.astype(bf16)
    logits_ref[...] = rows_dot(wr_ref[...], mixer_ref[...])
    for copy in first + second:
        copy.wait_send()


def mixer(inner, gate_in, w_low, w_state, w_dt, dt_bias, decay_rate, skip_gain, w_router):
    tokens, channels = inner.shape
    rank = w_low.shape[1]
    tiles = channels // LANES
    count, experts = lax.axis_size("seq"), lax.axis_size("exp")
    chunk = tokens // experts
    f32, bf16 = jnp.float32, jnp.bfloat16
    dma = pltpu.SemaphoreType.DMA
    any_spec = pl.BlockSpec(memory_space=pl.ANY)
    vmem_spec = pl.BlockSpec(memory_space=pltpu.VMEM)
    return pl.pallas_call(
        mixer_kernel,
        out_shape=(
            jax.ShapeDtypeStruct((tokens, channels), bf16),
            jax.ShapeDtypeStruct((NE, tokens), f32),
        ),
        in_specs=[vmem_spec] * 7 + [any_spec] * 2,
        out_specs=(vmem_spec, vmem_spec),
        scratch_shapes=[
            pltpu.VMEM(w_dt.shape, bf16),
            pltpu.VMEM((tokens, channels), bf16),
            pltpu.VMEM((tokens, channels), f32),
            pltpu.VMEM((experts, chunk, rank), f32),
            pltpu.VMEM((experts, chunk, LANES), f32),
            pltpu.VMEM((experts, chunk, rank), bf16),
            pltpu.VMEM((experts - 1, chunk, rank), bf16),
            pltpu.VMEM((experts - 1, chunk, LANES), f32),
            pltpu.VMEM((experts, chunk, rank), bf16),
            pltpu.VMEM((experts, chunk, LANES), f32),
        ]
        + [pltpu.VMEM((tokens * tiles, LANES), f32)] * 3
        + [pltpu.VMEM((tokens * N, LANES), f32)] * 2
        + [pltpu.VMEM((N * tiles, LANES), f32)]
        + [pltpu.VMEM((count, 2, 8, LANES), f32)] * 2
        + [pltpu.VMEM((count, 8, LANES), f32)] * 2
        + [dma((2,))] + [dma((2, experts))] * 4 + [dma((2,))] * 2,
        compiler_params=pltpu.CompilerParams(
            collective_id=1, has_side_effects=True, vmem_limit_bytes=VMEM_LIMIT),
    )(inner, w_low, w_state.T, dt_bias[None], decay_rate.T, skip_gain[None], w_router.T, w_dt, gate_in)


ROWS = 2 * CAP
WIDE = 1024
SIDE = 4


def expert_kernel(mixer_ref, logits_ref, ids_ref, gate_ref, up_ref, down_ref, out_ref,
                  x, w_in, w_out, acc, hid, hid_out, swap_out, swap_in, picked, logits_got, r1, r2, done, back,
                  w_sem, swap_sem, hop_send, hop_recv, logit_sem, back_send, back_recv, pass_send, pass_recv, ag_send, ag_recv, core_send, core_recv,
                  push_send, push_recv, hid_sem, r1_send, r1_recv, r2_send, r2_recv):
    seq, z = lax.axis_index("seq"), lax.axis_index("exp")
    experts = lax.axis_size("exp")
    tokens = mixer_ref.shape[0]
    c = seq % 2
    chip = seq // 2
    holder = z // 2
    f = gate_ref.shape[2]
    f32 = jnp.float32
    p1 = (1 - c) * (chip % SIDE) + c * (chip // SIDE)
    p2 = (1 - c) * (chip // SIDE) + c * (chip % SIDE)
    me = p2 * SIDE + p1

    def at(i1, i2, core=None):
        where = (1 - c) * (i2 * SIDE + i1) + c * (i1 * SIDE + i2)
        return {"seq": where * 2 + (c if core is None else core)}

    sibling = at(p1, p2, 1 - c)
    right1, left1 = at((p1 + 1) % SIDE, p2), at((p1 + 3) % SIDE, p2)
    right2, left2 = at(p1, (p2 + 1) % SIDE), at(p1, (p2 + 3) % SIDE)

    def remote(src, dst, send, recv, device):
        return pltpu.make_async_remote_copy(
            src_ref=src, dst_ref=dst, send_sem=send, recv_sem=recv,
            device_id=device, device_id_type=pl.DeviceIdType.MESH)

    def weights_in(o, n):
        return pltpu.make_async_copy(
            (gate_ref, up_ref)[n].at[0, pl.ds(o * WIDE, WIDE), :], w_in.at[o // 2, pl.ds((o % 2) * WIDE, WIDE), pl.ds(n * f, f)], w_sem.at[n, o])

    def weights_out(k):
        return pltpu.make_async_copy(
            down_ref.at[0, :, pl.ds((4 * c + k) * WIDE, WIDE)], w_out.at[k, pl.ds(0, f)], w_sem.at[2, k])

    def push(k):
        return remote(down_ref.at[0, :, pl.ds((4 * (1 - c) + k) * WIDE, WIDE)], w_out.at[k, pl.ds(f, f)],
                      push_send.at[k], push_recv.at[k], sibling)

    for o in range(8):
        for n in range(2):
            weights_in((4 * c + o) % 8, n).start()
    for k in range(4):
        weights_out(k).start()

    barrier = pltpu.get_barrier_semaphore()
    for peer in (sibling, right1, left1, right2, left2, at((p1 + 2) % SIDE, p2)):
        pl.semaphore_signal(barrier, inc=1, device_id=peer, device_id_type=pl.DeviceIdType.MESH)
    for core in range(2):
        for k in range(1, experts):
            peer = {"seq": chip * 2 + core, "exp": (z + k) % experts}
            pl.semaphore_signal(barrier, inc=1, device_id=peer, device_id_type=pl.DeviceIdType.MESH)

    spots = (experts * ROWS, tokens)
    row = lax.broadcasted_iota(jnp.int32, spots, 0)
    one, none = jnp.ones(spots, jnp.int32), jnp.zeros(spots, jnp.int32)
    expert = none
    for e in range(1, experts):
        expert = expert + jnp.where(row >= e * ROWS, one, none)
    row = row - ROWS * expert
    core_of = jnp.where(row >= CAP, one, none)
    slot = row - CAP * core_of
    named0 = jnp.broadcast_to(ids_ref[0:1, :], spots) == expert
    named1 = jnp.broadcast_to(ids_ref[1:2, :], spots) == expert
    load = jnp.where(named0 | named1, 1.0, 0.0)
    before = jnp.where(
        lax.broadcasted_iota(jnp.int32, (tokens, tokens), 0) < lax.broadcasted_iota(jnp.int32, (tokens, tokens), 1),
        1.0, 0.0).astype(jnp.bfloat16)
    earlier = jnp.dot(load.astype(jnp.bfloat16), before, preferred_element_type=f32)
    fits = (earlier == slot.astype(f32)) & (core_of == c)
    taken = jnp.where(fits, load, 0.0).astype(jnp.bfloat16)

    def picks(side):
        cols = pl.ds(pl.multiple_of(side * WIDE, WIDE), WIDE)
        return jnp.dot(taken, mixer_ref[:, cols], preferred_element_type=f32).astype(jnp.bfloat16).reshape(
            experts, ROWS, WIDE)

    swap_out[...] = picks(1 - c)
    pl.semaphore_wait(barrier, 6 + 2 * (experts - 1))
    swap = remote(swap_out, swap_in, swap_sem.at[0], swap_sem.at[1], sibling)
    swap.start()
    picked[...] = picks(c)
    swap.wait_recv()
    picked[...] = picked[...] + swap_in[...]

    piece = 2 * (z % 2) + c
    to_me = (1 - holder) * (chip) + holder * ((chip % SIDE) * SIDE + chip // SIDE)

    def hop(k):
        e = (z + k) % experts
        return remote(picked.at[e], x.at[holder, to_me, piece], hop_send.at[k], hop_recv.at[piece],
                      {"seq": chip * 2 + holder, "exp": e})

    for k in range(1, experts):
        hop(k).start()

    @pl.when(holder == c)
    def _():
        x[c, me, piece] = picked[z]

    @pl.when(holder != c)
    def _():
        hop(0).start()

    for k in range(4):
        push(k).start()
    logit_copies = []
    for k in range(1, experts):
        copy = remote(logits_ref, logits_got.at[k - 1], logit_sem.at[0, k], logit_sem.at[1, k],
                      {"exp": (z + k) % experts})
        copy.start()
        logit_copies.append(copy)
    early = (holder - c) * (holder - c)
    early = early * (1 - z % 2) + (1 - early) * (z % 2)

    def hop_arrive(side):
        for core in range(2):
            @pl.when((2 * c + side - z) * (2 * c + side - z) + (core - c) * (core - c) > 0)
            def _(core=core):
                part = x.at[c, me, 2 * side + core]
                remote(part, part, hop_send.at[0], hop_recv.at[2 * side + core], sibling).wait_recv()

    sent = []

    def spot(d1, d2):
        return ((p2 + 4 - d2) % SIDE) * SIDE + (p1 + 4 - d1) % SIDE

    def whole(d1, d2, n1, n2, device, slot):
        i = spot(d1, d2)
        copy = remote(x.at[c, i], x.at[c, i], ag_send.at[slot], ag_recv.at[n2 * 4 + n1, 0], device)
        copy.start()
        sent.append((ag_send, slot, 4))

    def pair(d1, d2, n1, n2, device, slot, k):
        i = spot(d1, d2)
        part = x.at[c, i, pl.ds(2 * k, 2)]
        copy = remote(part, part, ag_send.at[slot], ag_recv.at[n2 * 4 + n1, k], device)
        copy.start()
        sent.append((ag_send, slot, 2))

    def arrive(d1, d2):
        i = spot(d1, d2)
        if d2 == 2 or (d2 == 0 and d1 == 2):
            for k in range(2):
                part = x.at[c, i, pl.ds(2 * k, 2)]
                remote(part, part, ag_send.at[0], ag_recv.at[d2 * 4 + d1, k], sibling).wait_recv()
        else:
            remote(x.at[c, i], x.at[c, i], ag_send.at[0], ag_recv.at[d2 * 4 + d1, 0], sibling).wait_recv()

    def own_event():
        for side in (early, 1 - early):
            hop_arrive(side)
            part = x.at[c, me, pl.ds(2 * side, 2)]
            for device, slot, seen in ((right1, 16, 1), (left1, 17, 3), (right2, 0, 4), (left2, 4, 12)):
                remote(part, part, ag_send.at[slot], ag_recv.at[seen, 0], device).start()
            remote(part, part, core_send.at[0], core_recv.at[0], sibling).start()
        sent.extend([(ag_send, slot, 4) for slot in (16, 17, 0, 4)] + [(core_send, 0, 4)])

    def event(d1, d2):
        if (d1, d2) == (0, 0):
            own_event()
            return
        arrive(d1, d2)
        if d2 == 0:
            if d1 == 1:
                pair(1, 0, 2, 0, right1, 18, 0)
            elif d1 == 3:
                pair(3, 0, 2, 0, left1, 19, 1)
            whole(d1, 0, d1, 1, right2, d1)
            whole(d1, 0, d1, 3, left2, 4 + d1)
        elif d2 == 1:
            pair(d1, 1, d1, 2, right2, 8 + d1, 0)
        elif d2 == 3:
            pair(d1, 3, d1, 2, left2, 12 + d1, 1)
        i = spot(d1, d2)
        copy = remote(x.at[c, i], x.at[c, i], core_send.at[d2 * 4 + d1], core_recv.at[d2 * 4 + d1], sibling)
        copy.start()
        sent.append((core_send, d2 * 4 + d1, 4))

    def from_sibling(d2):
        for d1 in range(4):
            i = ((p1 + 4 - d2) % SIDE) * SIDE + (p2 + 4 - d1) % SIDE
            part = x.at[1 - c, i]
            remote(part, part, core_send.at[0], core_recv.at[d2 * 4 + d1], sibling).wait_recv()

    events = {
        0: [(0, 0), (1, 0), (3, 0), (0, 1), (0, 3), (2, 0)],
        1: [(1, 1), (1, 3)],
        2: [(3, 1), (3, 3)],
        3: [(2, 1), (2, 3)],
        6: [(0, 2)],
        8: [(1, 2)],
        10: [(3, 2)],
        12: [(2, 2)],
    }
    sibling_groups = {2: 0, 6: 1, 10: 3, 14: 2}

    @pl.loop(0, 16)
    def _(u):
        for when in range(16):
            if when in events or when in sibling_groups or when in (0, 2):
                @pl.when(u == when)
                def _(when=when):
                    for d1, d2 in events.get(when, ()):
                        event(d1, d2)
                    if when in (0, 2):
                        for k in range(4):
                            for n in range(2):
                                weights_in(4 * ((c + when // 2) % 2) + k, n).wait()
                    if when in sibling_groups:
                        from_sibling(sibling_groups[when])
        turn = u // 4
        d2 = turn + turn // 2 - 2 * (turn // 3)
        which = (u // 2) % 2
        half = (c + which) % 2
        base = (((1 - which) * p2 + which * p1 + 4 - d2) % SIDE) * SIDE

        side = u % 2
        rows = jnp.concatenate(
            [x[half, pl.ds(base, SIDE), 2 * side + k].reshape(SIDE * ROWS, WIDE) for k in range(2)], axis=1)
        part = jnp.dot(rows, w_in[half * 2 + side], preferred_element_type=f32).reshape(SIDE, ROWS, 2 * f)

        @pl.when(side == 0)
        def _():
            acc[which, pl.ds(base, SIDE)] = part

        @pl.when(side > 0)
        def _():
            acc[which, pl.ds(base, SIDE)] += part

    @pl.loop(0, 16)
    def _(i):
        flip = (i % SIDE) * SIDE + i // SIDE
        total = acc[0, i] + acc[1, flip]
        gated = total[:, :f]
        value = (gated / (1.0 + jnp.exp(-gated)) * total[:, f:]).astype(jnp.bfloat16)
        hid[0, i] = value
        hid_out[flip] = value
        remote(hid_out.at[flip], hid.at[1, flip], hid_sem.at[0], hid_sem.at[1], sibling).start()

    for sems, slot, size in sent:
        part = x.at[c, 0, pl.ds(0, size)]
        remote(part, part, sems.at[slot], ag_recv.at[0, 0], sibling).wait_send()
    for k in range(4):
        weights_out(k).wait()
        push(k).wait()
    remote(hid_out, hid.at[1], hid_sem.at[0], hid_sem.at[1], sibling).wait()

    def block(own, d, s):
        return (own + 3 - s) % SIDE if d == 0 else (own + 1 + s) % SIDE

    def r1_copy(s, d, jj):
        i = block(p2, d, s) * SIDE + block(p1, d, jj)
        return remote(x.at[c, i, pl.ds(2 * d, 2)], r1.at[s, d, jj], r1_send.at[s * 8 + d * 4 + jj],
                      r1_recv.at[s * 8 + d * 4 + jj], left2 if d else right2)

    def r2_copy(d, jj):
        i = p2 * SIDE + block(p1, d, jj)
        return remote(x.at[c, i, pl.ds(2 * d, 2)], r2.at[jj, d], r2_send.at[jj * 2 + d],
                      r2_recv.at[jj * 2 + d], at(block(p1, d, jj), p2))

    def back_copy(d, core):
        return remote(done.at[2 * d + core], back.at[z, core], back_send.at[2 * d + core], back_recv.at[z],
                      {"seq": chip * 2 + core, "exp": 2 * c + d})

    def is_me(d, core):
        return (2 * c + d - z) * (2 * c + d - z) + (core - c) * (core - c) == 0

    def give_back(d):
        for core in range(2):
            @pl.when(is_me(d, core))
            def _():
                back[z, core] = done[2 * d + core]

            @pl.when(jnp.logical_not(is_me(d, core)))
            def _():
                back_copy(d, core).start()

    def pass_copy(e, core):
        part = back.at[e, core]
        return remote(part, part, pass_send.at[e], pass_recv.at[e], sibling)

    for s in range(4):
        for d in range(2):
            base = block(p2, d, s) * SIDE

            @pl.loop(0, 2)
            def _(kk):
                k = 2 * d + kk
                rows = jnp.concatenate(
                    [hid[n, pl.ds(base, SIDE)].reshape(SIDE * ROWS, f) for n in range(2)], axis=1)
                part = jnp.dot(rows, w_out[k], preferred_element_type=f32)
                x[c, pl.ds(base, SIDE), k] = part.astype(jnp.bfloat16).reshape(SIDE, ROWS, WIDE)

            if s == 0:
                @pl.loop(0, 4)
                def _(jj):
                    r1_copy(0, d, jj).start()

        def turn(jj):
            for d in range(2):
                i = block(p2, d, s) * SIDE + block(p1, d, jj)
                if s > 0:
                    r1_copy(s - 1, d, jj).wait_recv()
                if s == 3 and jj == 3:
                    for other in range(3):
                        r2_copy(d, other).wait_recv()
                for kk in range(2 if s > 0 else 0):
                    k = 2 * d + kk
                    total = x[c, i, k].astype(f32) + r1[s - 1, d, jj, kk].astype(f32)
                    if s == 3 and jj == 3:
                        for other in range(3):
                            total = total + r2[other, d, kk].astype(f32)
                    if s == 3 and jj == 3:
                        done[k] = total.astype(jnp.bfloat16)
                    else:
                        x[c, i, k] = total.astype(jnp.bfloat16)
                if s < 3:
                    r1_copy(s, d, jj).start()
                elif jj < 3:
                    r2_copy(d, jj).start()
                else:
                    give_back(d)

        if s == 0:
            continue
        if s < 3:
            pl.loop(0, 4)(turn)
        else:
            for jj in range(4):
                turn(jj)

    for copy in logit_copies:
        copy.wait_recv()
    logits = logits_ref[...] + logits_got[0] + logits_got[1] + logits_got[2]
    listed = lax.broadcasted_iota(jnp.int32, logits.shape, 0)
    chosen = [
        jnp.sum(jnp.where(jnp.broadcast_to(ids_ref[k : k + 1, :], logits.shape) == listed, logits, 0.0), axis=0,
                keepdims=True)
        for k in range(2)
    ]
    shares = [1.0 / (1.0 + jnp.exp(chosen[1 - k] - chosen[k])) for k in range(2)]
    weight = jnp.where(fits & named0, jnp.broadcast_to(shares[0], spots), 0.0) + jnp.where(
        fits & named1, jnp.broadcast_to(shares[1], spots), 0.0)
    weight = weight.T
    weight_high = weight.astype(jnp.bfloat16)
    weight_low = (weight - weight_high.astype(f32)).astype(jnp.bfloat16)

    for k in range(experts):
        e = (z + k) % experts
        if k == 0:
            @pl.when(holder != c)
            def _():
                part = back.at[z, c]
                remote(part, part, back_send.at[0], back_recv.at[z], sibling).wait_recv()
        else:
            part = back.at[e, c]
            remote(part, part, back_send.at[0], back_recv.at[e], sibling).wait_recv()
        pass_copy(e, c).start()

    def combine(side):
        cols = pl.ds(pl.multiple_of(side * WIDE, WIDE), WIDE)
        rows = jnp.concatenate([back[e, side] for e in range(experts)], axis=0)
        out_ref[:, cols] = (
            mixer_ref[:, cols].astype(f32)
            + jnp.dot(weight_high, rows, preferred_element_type=f32)
            + jnp.dot(weight_low, rows, preferred_element_type=f32)
        )

    combine(c)
    for e in range(experts):
        pass_copy(e, 1 - c).wait_recv()
    combine(1 - c)

    swap.wait_send()
    for k in range(1, experts):
        hop(k).wait_send()

    @pl.when(holder != c)
    def _():
        hop(0).wait_send()

    for copy in logit_copies:
        copy.wait_send()
    for e in range(experts):
        pass_copy(e, c).wait_send()
    for d in range(2):
        for core in range(2):
            @pl.when(jnp.logical_not(is_me(d, core)))
            def _(d=d, core=core):
                back_copy(d, core).wait_send()
    for s in range(3):
        @pl.loop(0, 4)
        def _(jj):
            for d in range(2):
                r1_copy(s, d, jj).wait_send()
    for jj in range(3):
        for d in range(2):
            r2_copy(d, jj).wait_send()


def experts_layer(mixer_out, logits, ids, w_gate, w_up, w_down):
    f = w_gate.shape[2]
    experts = lax.axis_size("exp")
    bf16, f32 = jnp.bfloat16, jnp.float32
    dma = pltpu.SemaphoreType.DMA
    any_spec = pl.BlockSpec(memory_space=pl.ANY)
    vmem_spec = pl.BlockSpec(memory_space=pltpu.VMEM)
    return pl.pallas_call(
        expert_kernel,
        out_shape=jax.ShapeDtypeStruct(mixer_out.shape, f32),
        in_specs=[vmem_spec, vmem_spec, vmem_spec, any_spec, any_spec, any_spec],
        out_specs=vmem_spec,
        scratch_shapes=[
            pltpu.VMEM((2, 16, 4, ROWS, WIDE), bf16),
            pltpu.VMEM((4, 2 * WIDE, 2 * f), bf16),
            pltpu.VMEM((4, 2 * f, WIDE), bf16),
            pltpu.VMEM((2, 16, ROWS, 2 * f), f32),
            pltpu.VMEM((2, 16, ROWS, f), bf16),
            pltpu.VMEM((16, ROWS, f), bf16),
            pltpu.VMEM((experts, ROWS, WIDE), bf16),
            pltpu.VMEM((experts, ROWS, WIDE), bf16),
            pltpu.VMEM((experts, ROWS, WIDE), bf16),
            pltpu.VMEM((experts - 1,) + logits.shape, f32),
            pltpu.VMEM((3, 2, 4, 2, ROWS, WIDE), bf16),
            pltpu.VMEM((3, 2, 2, ROWS, WIDE), bf16),
            pltpu.VMEM((4, ROWS, WIDE), bf16),
            pltpu.VMEM((experts, 2, ROWS, WIDE), bf16),
            dma((3, 8)), dma((2,)), dma((4,)), dma((4,)), dma((2, 4)), dma((4,)), dma((4,)), dma((4,)), dma((4,)), dma((20,)), dma((16, 2)), dma((16,)), dma((16,)),
            dma((4,)), dma((4,)), dma((2,)), dma((24,)), dma((24,)), dma((6,)), dma((6,)),
        ],
        compiler_params=pltpu.CompilerParams(
            collective_id=0, has_side_effects=True, vmem_limit_bytes=VMEM_LIMIT),
        cost_estimate=pl.CostEstimate(flops=2 * 768 * 8192 * 384 * 3, bytes_accessed=20_000_000, transcendentals=300_000),
    )(mixer_out, logits, ids, w_gate, w_up, w_down)


def on_device(
    inner,
    gate_in,
    w_low,
    w_state,
    w_dt,
    dt_bias,
    decay_rate,
    skip_gain,
    w_router,
    expert_ids,
    w_gate,
    w_up,
    w_down,
):
    mixer_out, logits = mixer(
        inner, gate_in, w_low, w_state, w_dt, dt_bias, decay_rate, skip_gain, w_router
    )
    return experts_layer(mixer_out, logits, expert_ids.T, w_gate, w_up, w_down)


def solution(mesh):
    in_specs = (
        P("seq", "exp"),
        P("seq", "exp"),
        P("exp", None),
        P("exp", None),
        P(None, "exp"),
        P("exp"),
        P("exp", None),
        P("exp"),
        P("exp", None),
        P("seq", None),
        P("exp", None, "seq"),
        P("exp", None, "seq"),
        P("exp", "seq", None),
    )
    out_specs = P("seq", "exp")
    return jax.shard_map(
        on_device, mesh=mesh, in_specs=in_specs, out_specs=out_specs, check_vma=False
    )
```

```python
import functools

import jax
import jax.numpy as jnp
from jax import lax
from jax.experimental import pallas as pl
from jax.experimental.pallas import tpu as pltpu
from jax.sharding import PartitionSpec as P

N = 16
NE = 16
CAP = 24
LANES = 128
LOG2E = 1.4426950408889634
VMEM_LIMIT = 60 * 1024 * 1024


def softplus(v):
    return jnp.maximum(v, 0.0) + jnp.log1p(jnp.exp(-jnp.abs(v)))


def rows_dot(a, b):
    return lax.dot_general(a, b, (((1,), (1,)), ((), ())), preferred_element_type=jnp.float32)


def spread(ref, cols):
    tokens = cols.shape[0]
    for n in range(N):
        ref[pl.ds(n, tokens, stride=N), :] = jnp.broadcast_to(
            cols[:, n : n + 1], (tokens, LANES)
        )

def mixer_kernel(inner_ref, wlow_ref, wstate_ref, bias_ref, decay_ref, skip_ref, wr_ref, wdt_hbm, gate_hbm,
                 mixer_ref, logits_ref,
                 wdt, gate_s, silu_s, low_part, state_part, low_send, low_got, state_got, low_all, state_all,
                 dt_s, u_s, y_s, b_s, c_s, rate_s, ends, heard, carries, h0,
                 load_sem, low_sem, state_sem, low_sem2, state_sem2, end_sem, carry_sem):
    tokens, channels = inner_ref.shape
    tiles = channels // LANES
    count, experts = lax.axis_size("seq"), lax.axis_size("exp")
    seq, z = lax.axis_index("seq"), lax.axis_index("exp")
    chunk = tokens // experts
    f32, bf16 = jnp.float32, jnp.bfloat16
    mesh_ids = pl.DeviceIdType.MESH

    load_dt = pltpu.make_async_copy(wdt_hbm, wdt, load_sem.at[0])
    load_gate = pltpu.make_async_copy(gate_hbm, gate_s, load_sem.at[1])
    load_dt.start()
    load_gate.start()

    barrier = pltpu.get_barrier_semaphore()
    for k in range(1, experts):
        pl.semaphore_signal(barrier, inc=1, device_id={"exp": (z + k) % experts}, device_id_type=mesh_ids)

    @pl.loop(1, count)
    def _(k):
        pl.semaphore_signal(barrier, inc=1, device_id={"seq": (seq + k) % count}, device_id_type=mesh_ids)

    def remote(src, dst, send, recv, device):
        return pltpu.make_async_remote_copy(
            src_ref=src, dst_ref=dst, send_sem=send, recv_sem=recv, device_id=device, device_id_type=mesh_ids)

    values = inner_ref[...]
    low = jnp.dot(values, wlow_ref[...], preferred_element_type=f32)
    low_part[...] = low.reshape(low_part.shape)
    low_send[...] = low.astype(bf16).reshape(low_send.shape)
    state = rows_dot(values, wstate_ref[...])
    state_part[:, :, : 2 * N] = state.reshape(experts, chunk, 2 * N)
    state_part[:, :, 2 * N :] = jnp.zeros((experts, chunk, LANES - 2 * N), f32)
    for j in range(tiles):
        rate_s[pl.ds(j, N, stride=tiles), :] = decay_ref[:, pl.ds(j * LANES, LANES)] * -LOG2E
    pl.semaphore_wait(barrier, experts - 1 + count - 1)
    first = []
    for k in range(1, experts):
        to = (z + k) % experts
        first.append(remote(low_send.at[to], low_got.at[k - 1], low_sem.at[0, k], low_sem.at[1, k], {"exp": to}))
        first.append(remote(state_part.at[to], state_got.at[k - 1], state_sem.at[0, k], state_sem.at[1, k], {"exp": to}))
    for copy in first:
        copy.start()
    for copy in first:
        copy.wait_recv()
    low_sum, state_sum = low_part[z], state_part[z]
    for k in range(1, experts):
        low_sum = low_sum + low_got[k - 1].astype(f32)
        state_sum = state_sum + state_got[k - 1]
    low_all[z] = low_sum.astype(bf16)
    state_all[z] = state_sum
    second = []
    for k in range(1, experts):
        to = {"exp": (z + k) % experts}
        second.append(remote(low_all.at[z], low_all.at[z], low_sem2.at[0, k], low_sem2.at[1, k], to))
        second.append(remote(state_all.at[z], state_all.at[z], state_sem2.at[0, k], state_sem2.at[1, k], to))
    for copy in second:
        copy.start()
    for copy in second:
        copy.wait_recv()

    load_dt.wait()
    low_b = low_all[...].reshape(tokens, low_all.shape[2])
    for j in range(channels // 256):
        cols = pl.ds(j * 256, 256)
        dt = softplus(jnp.dot(low_b, wdt[:, cols], preferred_element_type=f32) + bias_ref[:, cols])
        u = dt * inner_ref[:, cols].astype(f32)
        for k in range(2):
            part = slice(k * LANES, (k + 1) * LANES)
            dt_s[pl.ds(2 * j + k, tokens, stride=tiles), :] = dt[:, part]
            u_s[pl.ds(2 * j + k, tokens, stride=tiles), :] = u[:, part]
    maps = state_all[...].reshape(tokens, LANES)
    spread(b_s, maps[:, :N])
    for half in range(2):
        rate = [rate_s[pl.ds(n * tiles + half * 8, 8), :] for n in range(N)]

        def step(t, carry):
            total, h = carry
            at = pl.multiple_of(t * tiles + half * 8, 8)
            dt = dt_s[pl.ds(at, 8), :]
            u = u_s[pl.ds(at, 8), :]
            new = []
            for n in range(N):
                b = b_s[pl.ds(t * N + n, 1), :]
                new.append(jnp.exp2(dt * rate[n]) * h[n] + u * b)
            return total + dt, tuple(new)

        zero = jnp.zeros((8, LANES), f32)
        total, h = lax.fori_loop(0, tokens, step, (zero, (zero,) * N), unroll=4)
        for n in range(N):
            ends[2 * n + half, 0] = jnp.exp2(total * rate[n])
            ends[2 * n + half, 1] = h[n]

        @pl.loop(0, count // 2)
        def _(k):
            to = (seq // 2 + k) % (count // 2) * 2 + half

            @pl.when(to != seq)
            def _():
                remote(ends.at[to], heard.at[seq], end_sem.at[0], end_sem.at[1], {"seq": to}).start()

    heard[seq] = ends[seq]
    spread(c_s, maps[:, N : 2 * N])
    others = pl.ds(0, count - 1)
    remote(ends.at[others], heard.at[others], end_sem.at[0], end_sem.at[1], {"seq": (seq + 1) % count}).wait_recv()

    def join(s, carry):
        carries[s] = carry
        return heard[s, 0] * carry + heard[s, 1]

    lax.fori_loop(0, count, join, jnp.zeros((8, LANES), f32), unroll=4)

    @pl.loop(1, count)
    def _(k):
        to = (seq + k) % count
        remote(carries.at[to], h0.at[seq], carry_sem.at[2], carry_sem.at[seq % 2], {"seq": to}).start()

    h0[seq] = carries[seq]

    for half in range(2):
        for own in range(2):
            @pl.when(seq % 2 == own)
            def _(half=half, own=own):
                group = pl.ds(0, count // 2 - (1 if own == half else 0))
                remote(carries.at[group], h0.at[group], carry_sem.at[2], carry_sem.at[half],
                       {"seq": (seq + 1) % count}).wait_recv()

        rate = [rate_s[pl.ds(n * tiles + half * 8, 8), :] for n in range(N)]

        def step(t, h):
            at = pl.multiple_of(t * tiles + half * 8, 8)
            dt = dt_s[pl.ds(at, 8), :]
            u = u_s[pl.ds(at, 8), :]
            new = []
            y = None
            for n in range(N):
                b = b_s[pl.ds(t * N + n, 1), :]
                c = c_s[pl.ds(t * N + n, 1), :]
                new.append(jnp.exp2(dt * rate[n]) * h[n] + u * b)
                y = new[n] * c if y is None else y + new[n] * c
            y_s[pl.ds(at, 8), :] = y
            return tuple(new)

        lax.fori_loop(0, tokens, step, tuple(h0[2 * n + half] for n in range(N)), unroll=4)
        if half == 0:
            load_gate.wait()
            for j in range(tiles):
                cols = pl.ds(j * LANES, LANES)
                gate = gate_s[:, cols].astype(f32)
                silu_s[:, cols] = gate / (1.0 + jnp.exp(-gate))
    for j in range(tiles):
        cols = pl.ds(j * LANES, LANES)
        y = y_s[pl.ds(j, tokens, stride=tiles), :]
        value = (y + skip_ref[:, cols] * inner_ref[:, cols].astype(f32)) * silu_s[:, cols]
        mixer_ref[:, cols] = value.astype(bf16)
    logits_ref[...] = rows_dot(wr_ref[...], mixer_ref[...])
    for copy in first + second:
        copy.wait_send()
    remote(ends.at[others], heard.at[others], end_sem.at[0], end_sem.at[1], {"seq": (seq + 1) % count}).wait_send()
    remote(carries.at[others], h0.at[others], carry_sem.at[2], carry_sem.at[0], {"seq": (seq + 1) % count}).wait_send()


def mixer(inner, gate_in, w_low, w_state, w_dt, dt_bias, decay_rate, skip_gain, w_router):
    tokens, channels = inner.shape
    rank = w_low.shape[1]
    tiles = channels // LANES
    count, experts = lax.axis_size("seq"), lax.axis_size("exp")
    chunk = tokens // experts
    f32, bf16 = jnp.float32, jnp.bfloat16
    dma = pltpu.SemaphoreType.DMA
    any_spec = pl.BlockSpec(memory_space=pl.ANY)
    vmem_spec = pl.BlockSpec(memory_space=pltpu.VMEM)
    return pl.pallas_call(
        mixer_kernel,
        out_shape=(
            jax.ShapeDtypeStruct((tokens, channels), bf16),
            jax.ShapeDtypeStruct((NE, tokens), f32),
        ),
        in_specs=[vmem_spec] * 7 + [any_spec] * 2,
        out_specs=(vmem_spec, vmem_spec),
        scratch_shapes=[
            pltpu.VMEM(w_dt.shape, bf16),
            pltpu.VMEM((tokens, channels), bf16),
            pltpu.VMEM((tokens, channels), f32),
            pltpu.VMEM((experts, chunk, rank), f32),
            pltpu.VMEM((experts, chunk, LANES), f32),
            pltpu.VMEM((experts, chunk, rank), bf16),
            pltpu.VMEM((experts - 1, chunk, rank), bf16),
            pltpu.VMEM((experts - 1, chunk, LANES), f32),
            pltpu.VMEM((experts, chunk, rank), bf16),
            pltpu.VMEM((experts, chunk, LANES), f32),
        ]
        + [pltpu.VMEM((tokens * tiles, LANES), f32)] * 3
        + [pltpu.VMEM((tokens * N, LANES), f32)] * 2
        + [pltpu.VMEM((N * tiles, LANES), f32)]
        + [pltpu.VMEM((count, 2, 8, LANES), f32)] * 2
        + [pltpu.VMEM((count, 8, LANES), f32)] * 2
        + [dma((2,))] + [dma((2, experts))] * 4 + [dma((2,)), dma((3,))],
        compiler_params=pltpu.CompilerParams(
            collective_id=1, has_side_effects=True, vmem_limit_bytes=VMEM_LIMIT),
    )(inner, w_low, w_state.T, dt_bias[None], decay_rate.T, skip_gain[None], w_router.T, w_dt, gate_in)


ROWS = 2 * CAP
WIDE = 1024
SIDE = 4


def expert_kernel(mixer_ref, logits_ref, ids_ref, gate_ref, up_ref, down_ref, out_ref,
                  x, w_in, w_out, acc, hid, hid_out, swap_out, swap_in, picked, logits_got, r1, r2, done, back,
                  w_sem, swap_sem, hop_send, hop_recv, logit_sem, back_send, back_recv, pass_send, pass_recv, ag_send, ag_recv, core_send, core_recv,
                  push_send, push_recv, hid_sem, r1_send, r1_recv, r2_send, r2_recv):
    seq, z = lax.axis_index("seq"), lax.axis_index("exp")
    experts = lax.axis_size("exp")
    tokens = mixer_ref.shape[0]
    c = seq % 2
    chip = seq // 2
    holder = z // 2
    f = gate_ref.shape[2]
    f32 = jnp.float32
    p1 = (1 - c) * (chip % SIDE) + c * (chip // SIDE)
    p2 = (1 - c) * (chip // SIDE) + c * (chip % SIDE)
    me = p2 * SIDE + p1

    def at(i1, i2, core=None):
        where = (1 - c) * (i2 * SIDE + i1) + c * (i1 * SIDE + i2)
        return {"seq": where * 2 + (c if core is None else core)}

    sibling = at(p1, p2, 1 - c)
    right1, left1 = at((p1 + 1) % SIDE, p2), at((p1 + 3) % SIDE, p2)
    right2, left2 = at(p1, (p2 + 1) % SIDE), at(p1, (p2 + 3) % SIDE)

    def remote(src, dst, send, recv, device):
        return pltpu.make_async_remote_copy(
            src_ref=src, dst_ref=dst, send_sem=send, recv_sem=recv,
            device_id=device, device_id_type=pl.DeviceIdType.MESH)

    def weights_in(o, n):
        return pltpu.make_async_copy(
            (gate_ref, up_ref)[n].at[0, pl.ds(o * WIDE, WIDE), :], w_in.at[o // 2, pl.ds((o % 2) * WIDE, WIDE), pl.ds(n * f, f)], w_sem.at[n, o])

    def weights_out(k):
        return pltpu.make_async_copy(
            down_ref.at[0, :, pl.ds((4 * c + k) * WIDE, WIDE)], w_out.at[k, pl.ds(0, f)], w_sem.at[2, k])

    def push(k):
        return remote(down_ref.at[0, :, pl.ds((4 * (1 - c) + k) * WIDE, WIDE)], w_out.at[k, pl.ds(f, f)],
                      push_send.at[k], push_recv.at[k], sibling)

    for o in range(8):
        for n in range(2):
            weights_in((4 * c + o) % 8, n).start()
    for k in range(4):
        weights_out(k).start()

    barrier = pltpu.get_barrier_semaphore()
    for peer in (sibling, right1, left1, right2, left2, at((p1 + 2) % SIDE, p2)):
        pl.semaphore_signal(barrier, inc=1, device_id=peer, device_id_type=pl.DeviceIdType.MESH)
    for core in range(2):
        for k in range(1, experts):
            peer = {"seq": chip * 2 + core, "exp": (z + k) % experts}
            pl.semaphore_signal(barrier, inc=1, device_id=peer, device_id_type=pl.DeviceIdType.MESH)

    spots = (experts * ROWS, tokens)
    row = lax.broadcasted_iota(jnp.int32, spots, 0)
    one, none = jnp.ones(spots, jnp.int32), jnp.zeros(spots, jnp.int32)
    expert = none
    for e in range(1, experts):
        expert = expert + jnp.where(row >= e * ROWS, one, none)
    row = row - ROWS * expert
    core_of = jnp.where(row >= CAP, one, none)
    slot = row - CAP * core_of
    named0 = jnp.broadcast_to(ids_ref[0:1, :], spots) == expert
    named1 = jnp.broadcast_to(ids_ref[1:2, :], spots) == expert
    load = jnp.where(named0 | named1, 1.0, 0.0)
    before = jnp.where(
        lax.broadcasted_iota(jnp.int32, (tokens, tokens), 0) < lax.broadcasted_iota(jnp.int32, (tokens, tokens), 1),
        1.0, 0.0).astype(jnp.bfloat16)
    earlier = jnp.dot(load.astype(jnp.bfloat16), before, preferred_element_type=f32)
    fits = (earlier == slot.astype(f32)) & (core_of == c)
    taken = jnp.where(fits, load, 0.0).astype(jnp.bfloat16)

    def picks(side):
        cols = pl.ds(pl.multiple_of(side * WIDE, WIDE), WIDE)
        return jnp.dot(taken, mixer_ref[:, cols], preferred_element_type=f32).astype(jnp.bfloat16).reshape(
            experts, ROWS, WIDE)

    swap_out[...] = picks(1 - c)
    pl.semaphore_wait(barrier, 6 + 2 * (experts - 1))
    swap = remote(swap_out, swap_in, swap_sem.at[0], swap_sem.at[1], sibling)
    swap.start()
    picked[...] = picks(c)
    swap.wait_recv()
    picked[...] = picked[...] + swap_in[...]

    piece = 2 * (z % 2) + c
    to_me = (1 - holder) * (chip) + holder * ((chip % SIDE) * SIDE + chip // SIDE)

    def hop(k):
        e = (z + k) % experts
        return remote(picked.at[e], x.at[holder, to_me, piece], hop_send.at[k], hop_recv.at[piece],
                      {"seq": chip * 2 + holder, "exp": e})

    for k in range(1, experts):
        hop(k).start()

    @pl.when(holder == c)
    def _():
        x[c, me, piece] = picked[z]

    @pl.when(holder != c)
    def _():
        hop(0).start()

    for k in range(4):
        push(k).start()
    logit_copies = []
    for k in range(1, experts):
        copy = remote(logits_ref, logits_got.at[k - 1], logit_sem.at[0, k], logit_sem.at[1, k],
                      {"exp": (z + k) % experts})
        copy.start()
        logit_copies.append(copy)
    early = (holder - c) * (holder - c)
    early = early * (1 - z % 2) + (1 - early) * (z % 2)

    def hop_arrive(side):
        for core in range(2):
            @pl.when((2 * c + side - z) * (2 * c + side - z) + (core - c) * (core - c) > 0)
            def _(core=core):
                part = x.at[c, me, 2 * side + core]
                remote(part, part, hop_send.at[0], hop_recv.at[2 * side + core], sibling).wait_recv()

    sent = []

    def spot(d1, d2):
        return ((p2 + 4 - d2) % SIDE) * SIDE + (p1 + 4 - d1) % SIDE

    def whole(d1, d2, n1, n2, device, slot):
        i = spot(d1, d2)
        copy = remote(x.at[c, i], x.at[c, i], ag_send.at[slot], ag_recv.at[n2 * 4 + n1, 0], device)
        copy.start()
        sent.append((ag_send, slot, 4))

    def pair(d1, d2, n1, n2, device, slot, k):
        i = spot(d1, d2)
        part = x.at[c, i, pl.ds(2 * k, 2)]
        copy = remote(part, part, ag_send.at[slot], ag_recv.at[n2 * 4 + n1, k], device)
        copy.start()
        sent.append((ag_send, slot, 2))

    def arrive(d1, d2):
        i = spot(d1, d2)
        if d2 == 2 or (d2 == 0 and d1 == 2):
            for k in range(2):
                part = x.at[c, i, pl.ds(2 * k, 2)]
                remote(part, part, ag_send.at[0], ag_recv.at[d2 * 4 + d1, k], sibling).wait_recv()
        else:
            remote(x.at[c, i], x.at[c, i], ag_send.at[0], ag_recv.at[d2 * 4 + d1, 0], sibling).wait_recv()

    def own_event():
        for side in (early, 1 - early):
            hop_arrive(side)
            part = x.at[c, me, pl.ds(2 * side, 2)]
            for device, slot, seen in ((right1, 16, 1), (left1, 17, 3), (right2, 0, 4), (left2, 4, 12)):
                remote(part, part, ag_send.at[slot], ag_recv.at[seen, 0], device).start()
            remote(part, part, core_send.at[0], core_recv.at[0], sibling).start()
        sent.extend([(ag_send, slot, 4) for slot in (16, 17, 0, 4)] + [(core_send, 0, 4)])

    def event(d1, d2):
        if (d1, d2) == (0, 0):
            own_event()
            return
        arrive(d1, d2)
        if d2 == 0:
            if d1 == 1:
                pair(1, 0, 2, 0, right1, 18, 0)
            elif d1 == 3:
                pair(3, 0, 2, 0, left1, 19, 1)
            whole(d1, 0, d1, 1, right2, d1)
            whole(d1, 0, d1, 3, left2, 4 + d1)
        elif d2 == 1:
            pair(d1, 1, d1, 2, right2, 8 + d1, 0)
        elif d2 == 3:
            pair(d1, 3, d1, 2, left2, 12 + d1, 1)
        i = spot(d1, d2)
        copy = remote(x.at[c, i], x.at[c, i], core_send.at[d2 * 4 + d1], core_recv.at[d2 * 4 + d1], sibling)
        copy.start()
        sent.append((core_send, d2 * 4 + d1, 4))

    def from_sibling(d2):
        for d1 in range(4):
            i = ((p1 + 4 - d2) % SIDE) * SIDE + (p2 + 4 - d1) % SIDE
            part = x.at[1 - c, i]
            remote(part, part, core_send.at[0], core_recv.at[d2 * 4 + d1], sibling).wait_recv()

    events = {
        0: [(0, 0), (1, 0), (3, 0), (0, 1), (0, 3), (2, 0)],
        1: [(1, 1), (1, 3)],
        2: [(3, 1), (3, 3)],
        3: [(2, 1), (2, 3)],
        6: [(0, 2)],
        8: [(1, 2)],
        10: [(3, 2)],
        12: [(2, 2)],
    }
    sibling_groups = {2: 0, 6: 1, 10: 3, 14: 2}

    @pl.loop(0, 16)
    def _(u):
        for when in range(16):
            if when in events or when in sibling_groups or when in (0, 2):
                @pl.when(u == when)
                def _(when=when):
                    for d1, d2 in events.get(when, ()):
                        event(d1, d2)
                    if when in (0, 2):
                        for k in range(4):
                            for n in range(2):
                                weights_in(4 * ((c + when // 2) % 2) + k, n).wait()
                    if when in sibling_groups:
                        from_sibling(sibling_groups[when])
        turn = u // 4
        d2 = turn + turn // 2 - 2 * (turn // 3)
        which = (u // 2) % 2
        half = (c + which) % 2
        base = (((1 - which) * p2 + which * p1 + 4 - d2) % SIDE) * SIDE

        side = u % 2
        rows = jnp.concatenate(
            [x[half, pl.ds(base, SIDE), 2 * side + k].reshape(SIDE * ROWS, WIDE) for k in range(2)], axis=1)
        part = jnp.dot(rows, w_in[half * 2 + side], preferred_element_type=f32).reshape(SIDE, ROWS, 2 * f)

        @pl.when(side == 0)
        def _():
            acc[which, pl.ds(base, SIDE)] = part

        @pl.when(side > 0)
        def _():
            acc[which, pl.ds(base, SIDE)] += part

    @pl.loop(0, 16)
    def _(i):
        flip = (i % SIDE) * SIDE + i // SIDE
        total = acc[0, i] + acc[1, flip]
        gated = total[:, :f]
        value = (gated / (1.0 + jnp.exp(-gated)) * total[:, f:]).astype(jnp.bfloat16)
        hid[0, i] = value
        hid_out[flip] = value
        remote(hid_out.at[flip], hid.at[1, flip], hid_sem.at[0], hid_sem.at[1], sibling).start()

    for sems, slot, size in sent:
        part = x.at[c, 0, pl.ds(0, size)]
        remote(part, part, sems.at[slot], ag_recv.at[0, 0], sibling).wait_send()
    for k in range(4):
        weights_out(k).wait()
        push(k).wait()
    remote(hid_out, hid.at[1], hid_sem.at[0], hid_sem.at[1], sibling).wait()

    def block(own, d, s):
        return (own + 3 - s) % SIDE if d == 0 else (own + 1 + s) % SIDE

    def r1_copy(s, d, jj):
        i = block(p2, d, s) * SIDE + block(p1, d, jj)
        return remote(x.at[c, i, pl.ds(2 * d, 2)], r1.at[s, d, jj], r1_send.at[s * 8 + d * 4 + jj],
                      r1_recv.at[s * 8 + d * 4 + jj], left2 if d else right2)

    def r2_copy(d, jj):
        i = p2 * SIDE + block(p1, d, jj)
        return remote(x.at[c, i, pl.ds(2 * d, 2)], r2.at[jj, d], r2_send.at[jj * 2 + d],
                      r2_recv.at[jj * 2 + d], at(block(p1, d, jj), p2))

    def back_copy(d, core):
        return remote(done.at[2 * d + core], back.at[z, core], back_send.at[2 * d + core], back_recv.at[z],
                      {"seq": chip * 2 + core, "exp": 2 * c + d})

    def is_me(d, core):
        return (2 * c + d - z) * (2 * c + d - z) + (core - c) * (core - c) == 0

    def give_back(d):
        for core in range(2):
            @pl.when(is_me(d, core))
            def _():
                back[z, core] = done[2 * d + core]

            @pl.when(jnp.logical_not(is_me(d, core)))
            def _():
                back_copy(d, core).start()

    def pass_copy(e, core):
        part = back.at[e, core]
        return remote(part, part, pass_send.at[e], pass_recv.at[e], sibling)

    for s in range(4):
        for d in range(2):
            base = block(p2, d, s) * SIDE

            @pl.loop(0, 2)
            def _(kk):
                k = 2 * d + kk
                rows = jnp.concatenate(
                    [hid[n, pl.ds(base, SIDE)].reshape(SIDE * ROWS, f) for n in range(2)], axis=1)
                part = jnp.dot(rows, w_out[k], preferred_element_type=f32)
                x[c, pl.ds(base, SIDE), k] = part.astype(jnp.bfloat16).reshape(SIDE, ROWS, WIDE)

            if s == 0:
                @pl.loop(0, 4)
                def _(jj):
                    r1_copy(0, d, jj).start()

        def turn(jj):
            for d in range(2):
                i = block(p2, d, s) * SIDE + block(p1, d, jj)
                if s > 0:
                    r1_copy(s - 1, d, jj).wait_recv()
                if s == 3 and jj == 3:
                    for other in range(3):
                        r2_copy(d, other).wait_recv()
                for kk in range(2 if s > 0 else 0):
                    k = 2 * d + kk
                    total = x[c, i, k].astype(f32) + r1[s - 1, d, jj, kk].astype(f32)
                    if s == 3 and jj == 3:
                        for other in range(3):
                            total = total + r2[other, d, kk].astype(f32)
                    if s == 3 and jj == 3:
                        done[k] = total.astype(jnp.bfloat16)
                    else:
                        x[c, i, k] = total.astype(jnp.bfloat16)
                if s < 3:
                    r1_copy(s, d, jj).start()
                elif jj < 3:
                    r2_copy(d, jj).start()
                else:
                    give_back(d)

        if s == 0:
            continue
        if s < 3:
            pl.loop(0, 4)(turn)
        else:
            for jj in range(4):
                turn(jj)

    for copy in logit_copies:
        copy.wait_recv()
    logits = logits_ref[...] + logits_got[0] + logits_got[1] + logits_got[2]
    listed = lax.broadcasted_iota(jnp.int32, logits.shape, 0)
    chosen = [
        jnp.sum(jnp.where(jnp.broadcast_to(ids_ref[k : k + 1, :], logits.shape) == listed, logits, 0.0), axis=0,
                keepdims=True)
        for k in range(2)
    ]
    shares = [1.0 / (1.0 + jnp.exp(chosen[1 - k] - chosen[k])) for k in range(2)]
    weight = jnp.where(fits & named0, jnp.broadcast_to(shares[0], spots), 0.0) + jnp.where(
        fits & named1, jnp.broadcast_to(shares[1], spots), 0.0)
    weight = weight.T
    weight_high = weight.astype(jnp.bfloat16)
    weight_low = (weight - weight_high.astype(f32)).astype(jnp.bfloat16)

    for k in range(experts):
        e = (z + k) % experts
        if k == 0:
            @pl.when(holder != c)
            def _():
                part = back.at[z, c]
                remote(part, part, back_send.at[0], back_recv.at[z], sibling).wait_recv()
        else:
            part = back.at[e, c]
            remote(part, part, back_send.at[0], back_recv.at[e], sibling).wait_recv()
        pass_copy(e, c).start()

    def combine(side):
        cols = pl.ds(pl.multiple_of(side * WIDE, WIDE), WIDE)
        rows = jnp.concatenate([back[e, side] for e in range(experts)], axis=0)
        out_ref[:, cols] = (
            mixer_ref[:, cols].astype(f32)
            + jnp.dot(weight_high, rows, preferred_element_type=f32)
            + jnp.dot(weight_low, rows, preferred_element_type=f32)
        )

    combine(c)
    for e in range(experts):
        pass_copy(e, 1 - c).wait_recv()
    combine(1 - c)

    swap.wait_send()
    for k in range(1, experts):
        hop(k).wait_send()

    @pl.when(holder != c)
    def _():
        hop(0).wait_send()

    for copy in logit_copies:
        copy.wait_send()
    for e in range(experts):
        pass_copy(e, c).wait_send()
    for d in range(2):
        for core in range(2):
            @pl.when(jnp.logical_not(is_me(d, core)))
            def _(d=d, core=core):
                back_copy(d, core).wait_send()
    for s in range(3):
        @pl.loop(0, 4)
        def _(jj):
            for d in range(2):
                r1_copy(s, d, jj).wait_send()
    for jj in range(3):
        for d in range(2):
            r2_copy(d, jj).wait_send()


def experts_layer(mixer_out, logits, ids, w_gate, w_up, w_down):
    f = w_gate.shape[2]
    experts = lax.axis_size("exp")
    bf16, f32 = jnp.bfloat16, jnp.float32
    dma = pltpu.SemaphoreType.DMA
    any_spec = pl.BlockSpec(memory_space=pl.ANY)
    vmem_spec = pl.BlockSpec(memory_space=pltpu.VMEM)
    return pl.pallas_call(
        expert_kernel,
        out_shape=jax.ShapeDtypeStruct(mixer_out.shape, f32),
        in_specs=[vmem_spec, vmem_spec, vmem_spec, any_spec, any_spec, any_spec],
        out_specs=vmem_spec,
        scratch_shapes=[
            pltpu.VMEM((2, 16, 4, ROWS, WIDE), bf16),
            pltpu.VMEM((4, 2 * WIDE, 2 * f), bf16),
            pltpu.VMEM((4, 2 * f, WIDE), bf16),
            pltpu.VMEM((2, 16, ROWS, 2 * f), f32),
            pltpu.VMEM((2, 16, ROWS, f), bf16),
            pltpu.VMEM((16, ROWS, f), bf16),
            pltpu.VMEM((experts, ROWS, WIDE), bf16),
            pltpu.VMEM((experts, ROWS, WIDE), bf16),
            pltpu.VMEM((experts, ROWS, WIDE), bf16),
            pltpu.VMEM((experts - 1,) + logits.shape, f32),
            pltpu.VMEM((3, 2, 4, 2, ROWS, WIDE), bf16),
            pltpu.VMEM((3, 2, 2, ROWS, WIDE), bf16),
            pltpu.VMEM((4, ROWS, WIDE), bf16),
            pltpu.VMEM((experts, 2, ROWS, WIDE), bf16),
            dma((3, 8)), dma((2,)), dma((4,)), dma((4,)), dma((2, 4)), dma((4,)), dma((4,)), dma((4,)), dma((4,)), dma((20,)), dma((16, 2)), dma((16,)), dma((16,)),
            dma((4,)), dma((4,)), dma((2,)), dma((24,)), dma((24,)), dma((6,)), dma((6,)),
        ],
        compiler_params=pltpu.CompilerParams(
            collective_id=0, has_side_effects=True, vmem_limit_bytes=VMEM_LIMIT),
        cost_estimate=pl.CostEstimate(flops=2 * 768 * 8192 * 384 * 3, bytes_accessed=20_000_000, transcendentals=300_000),
    )(mixer_out, logits, ids, w_gate, w_up, w_down)


def on_device(
    inner,
    gate_in,
    w_low,
    w_state,
    w_dt,
    dt_bias,
    decay_rate,
    skip_gain,
    w_router,
    expert_ids,
    w_gate,
    w_up,
    w_down,
):
    mixer_out, logits = mixer(
        inner, gate_in, w_low, w_state, w_dt, dt_bias, decay_rate, skip_gain, w_router
    )
    return experts_layer(mixer_out, logits, expert_ids.T, w_gate, w_up, w_down)


def solution(mesh):
    in_specs = (
        P("seq", "exp"),
        P("seq", "exp"),
        P("exp", None),
        P("exp", None),
        P(None, "exp"),
        P("exp"),
        P("exp", None),
        P("exp"),
        P("exp", None),
        P("seq", None),
        P("exp", None, "seq"),
        P("exp", None, "seq"),
        P("exp", "seq", None),
    )
    out_specs = P("seq", "exp")
    return jax.shard_map(
        on_device, mesh=mesh, in_specs=in_specs, out_specs=out_specs, check_vma=False
    )
```
